32 devices in a mesh: fsdp: 8 (over y, x, core), sp: 4 (over z).
Axes of the slice: x: 2, y: 2, z: 4, core: 2. Of those that a mesh axis runs over, the one named last changes fastest.
Arguments:
- tokens: bfloat16 [12288, 1536], P(('fsdp', 'sp')), may hold values from -6 to 6
- cotangent: bfloat16 [12288, 1536], P(('fsdp', 'sp')), may hold values from -6 to 6
- seq_lengths: int32 [8], P('fsdp'), may hold values from 1024 to 1536, as said below
- block_order: int32 [8, 8], P('fsdp'), may hold values from 0 to 7, as said below
- w_query: bfloat16 [1536, 1536], P('fsdp'), may hold values from -0.15625 to 0.15625
- w_key: bfloat16 [1536, 256], P('fsdp'), may hold values from -0.15625 to 0.15625
- w_value: bfloat16 [1536, 256], P('fsdp'), may hold values from -0.15625 to 0.15625
- b_query: bfloat16 [1536], P('fsdp'), may hold values from -3 to 3
- b_key: bfloat16 [256], P('fsdp'), may hold values from -3 to 3
- b_value: bfloat16 [256], P('fsdp'), may hold values from -3 to 3
- w_output: bfloat16 [1536, 1536], P('fsdp'), may hold values from -1.25 to 1.25
- gain_attn: bfloat16 [1536], P('fsdp'), may hold values from 0.5 to 1.5
- gain_mlp: bfloat16 [1536], P('fsdp'), may hold values from 0.5 to 1.5
- w_gate: bfloat16 [1536, 8960], P('fsdp'), may hold values from -0.15625 to 0.15625
- w_up: bfloat16 [1536, 8960], P('fsdp'), may hold values from -0.15625 to 0.15625
- w_down: bfloat16 [8960, 1536], P('fsdp'), may hold values from -0.0625 to 0.0625
Outputs:
- layer_out: bfloat16 [12288, 1536], P(('fsdp', 'sp'))
- input_grad: float32 [12288, 1536], P(('fsdp', 'sp'))
- grad_w_query: float32 [1536, 1536], P('fsdp')
- grad_w_key: float32 [1536, 256], P('fsdp')
- grad_w_value: float32 [1536, 256], P('fsdp')
- grad_b_query: float32 [1536], P('fsdp')
- grad_b_key: float32 [256], P('fsdp')
- grad_b_value: float32 [256], P('fsdp')
- grad_w_output: float32 [1536, 1536], P('fsdp')
- grad_gain_attn: float32 [1536], P('fsdp')
- grad_gain_mlp: float32 [1536], P('fsdp')
- grad_w_gate: float32 [1536, 8960], P('fsdp')
- grad_w_up: float32 [1536, 8960], P('fsdp')
- grad_w_down: float32 [8960, 1536], P('fsdp')
- root_means: float32 [3], replicated
The draws below stay inside these ranges and needn't reach their ends.
Inputs may be any that keep to these rules, and one draw needn't show every extreme that they name: Each group's sequence fills the first seq_lengths[f] places of its packed stream; the rest is padding. Some group is full and some group has exactly 1024. `block_order`: each row is a permutation of the group's 8 stream blocks; entries 2s and 2s + 1 are b and 7 - b for some b.
All inputs are finite; a program needn't handle non-finite values.
Results may differ from the reference program's by a relative error of at most 0.023.
Values may be sent and summed in bfloat16 or wider, within the bound.
No kernel may reach another device: no remote copies, remote signals or barrier semaphores. Data moves between devices by JAX's collectives and lax.ppermute only.
A program may use at most 576 MiB of HBM per device.

```python
import jax
import jax.numpy as jnp
from jax import lax

D = 1536
H = 12
KVH = 2
HD = 128
FF = 8960
MIN_LEN = 1024
G = 1536
BLOCK = 192
BLOCKS = 8
QB = 512
HQ = 1536
KVD = 256
TOKENS = 12288
N_FSDP = 8
N_SP = 4


def draw_seq_lengths(key, part):
    key = jax.random.fold_in(key, 11)
    key_len, key_pick = jax.random.split(key)
    lengths = jax.random.randint(key_len, (N_FSDP,), MIN_LEN, G + 1)
    chosen = jax.random.permutation(key_pick, N_FSDP)
    lengths = lengths.at[chosen[0]].set(G)
    lengths = lengths.at[chosen[1]].set(MIN_LEN)
    return lengths.astype(jnp.int32)


def draw_block_order(key, part):
    key = jax.random.fold_in(key, 23)

    def one_group(group_key):
        key_pairs, key_flip = jax.random.split(group_key)
        pair_ids = jax.random.permutation(key_pairs, N_SP)
        flip_bits = jax.random.randint(key_flip, (N_SP,), 0, 2)
        first_block = jnp.where(flip_bits == 0, pair_ids, BLOCKS - 1 - pair_ids)
        second_block = BLOCKS - 1 - first_block
        return jnp.stack([first_block, second_block], axis=1).reshape(BLOCKS)
    return jax.vmap(one_group)(jax.random.split(key, N_FSDP)).astype(jnp.int32)


def shard_levels(stream_key, dims, shards, least, largest):
    factor_of, own = 1.0, jax.random.fold_in(stream_key, 6)
    for dim, shards_of in shards:
        steps = jnp.exp(jax.random.uniform(jax.random.fold_in(own, dim), (shards_of,), jnp.float32, least / len(shards), largest / len(shards)))
        factor_of = factor_of * jnp.repeat(steps, dims[dim] // shards_of).reshape([-1 if axis == dim else 1 for axis in range(len(dims))])
    return factor_of


def scatter_about(stream_key, extent, scale, reach, shards=(), kind=jnp.bfloat16):
    array = jax.random.normal(stream_key, extent, jnp.float32) * scale
    if len(shards) > 0:
        array = shard_levels(stream_key, extent, shards, -0.22, 0.18) * array
    return jnp.clip(array, min=-reach, max=reach).astype(kind)


def setup_inputs(seed: int = 0) -> dict:
    key_list = jax.random.split(jax.random.key(seed), 17)
    return {
        "tokens": scatter_about(key_list[0], (TOKENS, D), 1.0, 6.0, ((0, 32),)),
        "cotangent": scatter_about(key_list[1], (TOKENS, D), 1.0, 6.0, ((0, 32),)),
        "seq_lengths": draw_seq_lengths(jax.random.fold_in(key_list[16], 71), 0),
        "block_order": draw_block_order(jax.random.fold_in(key_list[16], 71), 0),
        "w_query": scatter_about(key_list[4], (D, HQ), D ** -0.5, 0.15625, ((0, 8),)),
        "w_key": scatter_about(key_list[5], (D, KVD), D ** -0.5, 0.15625, ((0, 8),)),
        "w_value": scatter_about(key_list[6], (D, KVD), D ** -0.5, 0.15625, ((0, 8),)),
        "b_query": scatter_about(key_list[7], (HQ,), 0.5, 3.0, ((0, 8),)),
        "b_key": scatter_about(key_list[8], (KVD,), 0.5, 3.0, ((0, 8),)),
        "b_value": scatter_about(key_list[9], (KVD,), 0.5, 3.0, ((0, 8),)),
        "w_output": scatter_about(key_list[10], (HQ, D), (HQ // 64) ** -0.5, 1.25, ((0, 8),)),
        "gain_attn": jnp.clip(1.0 + 0.1 * jax.random.normal(key_list[11], (D,), jnp.float32), 0.5, 1.5).astype(jnp.bfloat16),
        "gain_mlp": jnp.clip(1.0 + 0.1 * jax.random.normal(key_list[12], (D,), jnp.float32), 0.5, 1.5).astype(jnp.bfloat16),
        "w_gate": scatter_about(key_list[13], (D, FF), D ** -0.5, 0.15625, ((0, 8),)),
        "w_up": scatter_about(key_list[14], (D, FF), D ** -0.5, 0.15625, ((0, 8),)),
        "w_down": scatter_about(key_list[15], (FF, D), FF ** -0.5, 0.0625, ((0, 8),)),
    }


EPS = 1e-06
THETA = 1000000.0
HIGHEST = lax.Precision.HIGHEST

@jax.custom_vjp
def low(v):
    return lax.optimization_barrier(v.astype(jnp.bfloat16)).astype(jnp.float32)

@jax.custom_vjp
def low_back(v):
    return v

def low_keep(v):
    return (low(v), None)

def low_pass(kept, grad):
    return (grad,)

def back_keep(v):
    return (v, None)

def back_low(kept, grad):
    return (low(grad),)
low.defvjp(low_keep, low_pass)
low_back.defvjp(back_keep, back_low)

def rotary_tables(positions):
    half_width = HD // 2
    inverse = THETA ** (-(jnp.arange(half_width, dtype=jnp.float32) * 2.0) / HD)
    angles = positions.astype(jnp.float32)[:, None] * inverse[None, :]
    angles = jnp.concatenate([angles, angles], axis=-1)
    return (jnp.cos(angles), jnp.sin(angles))

def rotate(values, cosine, sine):
    half_width = values.shape[-1] // 2
    turned = jnp.concatenate([-values[..., half_width:], values[..., :half_width]], axis=-1)
    return values * cosine[:, None, :] + turned * sine[:, None, :]

def stream_positions(order_row):
    row_ids = jnp.arange(G, dtype=jnp.int32)
    return order_row[row_ids // BLOCK] * BLOCK + row_ids % BLOCK

def product(left, right):
    return jnp.dot(left, right, precision=HIGHEST)

def rms_norm(values, gain):
    return values * lax.rsqrt(lax.optimization_barrier(jnp.mean(values * values, axis=-1, keepdims=True)) + EPS) * gain

def group_attention(queries, keys_in, values_in, positions):
    repeat_by = H // KVH
    keys_all = jnp.repeat(keys_in, repeat_by, axis=1)
    values_all = jnp.repeat(values_in, repeat_by, axis=1)
    scaling = HD ** (-0.5)

    def one_block(pieces):
        block_q, block_pos = pieces
        scores = low_back(jnp.einsum('qhd,khd->hqk', block_q, keys_all, precision=HIGHEST) * scaling)
        allowed = positions[None, None, :] <= block_pos[None, :, None]
        scores = jnp.where(allowed, scores, -1e+30)
        row_peak = lax.optimization_barrier(jnp.max(scores, axis=-1, keepdims=True))
        weights_exp = jnp.exp(scores - row_peak)
        probabilities = weights_exp / lax.optimization_barrier(jnp.sum(weights_exp, axis=-1, keepdims=True))
        return jnp.einsum('hqk,khd->qhd', low(probabilities), values_all, precision=HIGHEST)
    blocks = G // QB
    outputs = lax.map(jax.checkpoint(one_block), (queries.reshape(blocks, QB, H, HD), positions.reshape(blocks, QB)))
    return outputs.reshape(G, H * HD)

def group_layer(weights_all, inputs, positions, valid_rows):
    w_query, w_key, w_value, b_query, b_key, b_value, w_output, gain_attn, gain_mlp, w_gate, w_up, w_down = weights_all
    cosine, sine = rotary_tables(positions)
    normed_one = low(rms_norm(inputs, gain_attn))
    query_lin = low_back(product(normed_one, w_query) + b_query)
    key_lin = low_back(product(normed_one, w_key) + b_key)
    value_lin = low_back(product(normed_one, w_value) + b_value)
    query_rot = low(rotate(query_lin.reshape(G, H, HD), cosine, sine))
    key_rot = low(rotate(key_lin.reshape(G, KVH, HD), cosine, sine))
    value_low = low(value_lin.reshape(G, KVH, HD))
    mixed = low(low_back(group_attention(query_rot, key_rot, value_low, positions)))
    attn_branch = low_back(product(mixed, w_output))
    hidden_in = inputs + valid_rows * attn_branch
    normed_two = low(rms_norm(hidden_in, gain_mlp))
    gate_lin = low_back(product(normed_two, w_gate))
    up_lin = low_back(product(normed_two, w_up))
    hidden = low(gate_lin * jax.nn.sigmoid(gate_lin) * up_lin)
    mlp_branch = low_back(product(hidden, w_down))
    return (hidden_in + valid_rows * mlp_branch, attn_branch, mlp_branch)

def reference(tokens, cotangent, seq_lengths, block_order, w_query, w_key, w_value, b_query, b_key, b_value, w_output, gain_attn, gain_mlp, w_gate, w_up, w_down):
    positions = jax.vmap(stream_positions)(block_order)
    valid_rows = (positions < seq_lengths[:, None]).astype(jnp.float32)[..., None]
    floats = [item.astype(jnp.float32) for item in (tokens, w_query, w_key, w_value, b_query, b_key, b_value, w_output, gain_attn, gain_mlp, w_gate, w_up, w_down)]

    def whole(inputs, *weights_all):

        def group_step(carried, pieces):
            produced = jax.checkpoint(group_layer)(weights_all, pieces[0], pieces[1], pieces[2])
            return (carried, produced)
        unused, produced = lax.scan(group_step, jnp.zeros((), jnp.float32), (inputs.reshape(N_FSDP, G, D), positions, valid_rows))
        return (produced[0].reshape(TOKENS, D), (produced[1].reshape(TOKENS, D), produced[2].reshape(TOKENS, D)))
    result, pullback, branches = jax.vjp(whole, *floats, has_aux=True)
    gradients = pullback(cotangent.astype(jnp.float32))
    valid_flat = valid_rows.reshape(TOKENS, 1)
    count_valid = jnp.sum(valid_flat) * D
    root_means = jnp.stack([jnp.sqrt(jnp.sum(valid_flat * result * result) / count_valid), jnp.sqrt(jnp.sum(valid_flat * branches[0] * branches[0]) / count_valid), jnp.sqrt(jnp.sum(valid_flat * branches[1] * branches[1]) / count_valid)])
    return (result.astype(jnp.bfloat16), gradients[0], gradients[1], gradients[2], gradients[3], gradients[4], gradients[5], gradients[6], gradients[7], gradients[8], gradients[9], gradients[10], gradients[11], gradients[12], root_means)
```

```python
import functools

import jax
import jax.numpy as jnp
from jax import lax
from jax.experimental import pallas as pl
from jax.experimental.pallas import tpu as pltpu
from jax.sharding import PartitionSpec as P

H = 12
KVH = 2
HD = 128
HEADS_STEP = 2


EPS = 1e-06
THETA = 1000000.0
BF = jnp.bfloat16
F32 = jnp.float32


def rotary_tables(positions):
    half_width = HD // 2
    inverse = THETA ** (-(jnp.arange(half_width, dtype=F32) * 2.0) / HD)
    angles = positions.astype(F32)[:, None] * inverse[None, :]
    cosine, sine = jnp.cos(angles), jnp.sin(angles)
    return (
        jnp.concatenate([cosine, cosine], axis=-1),
        jnp.concatenate([-sine, sine], axis=-1),
    )


def swap_halves(values):
    half_width = HD // 2
    return jnp.concatenate([values[..., half_width:], values[..., :half_width]], axis=-1)


def stream_positions(order_row, first_row, row_count, block_size):
    row_ids = first_row + jnp.arange(row_count, dtype=jnp.int32)
    which_block = row_ids // block_size
    matches = jnp.arange(order_row.shape[0], dtype=jnp.int32)[None, :] == which_block[:, None]
    block_start = jnp.sum(jnp.where(matches, order_row[None, :], 0), axis=1)
    return block_start * block_size + row_ids % block_size


def norm_backward(normed_grad, unit_rows, gain_rows, scale_rows):
    gain_grad = jnp.sum(normed_grad * unit_rows, axis=0)
    scaled = normed_grad * gain_rows
    inner = jnp.mean(scaled * unit_rows, axis=-1, keepdims=True)
    return (gain_grad, scale_rows * (scaled - unit_rows * inner))


def contract_last(left, right):
    return lax.dot_general(left, right, (((1,), (1,)), ((), ())), preferred_element_type=F32)


def contract_first(left, right):
    return lax.dot_general(left, right, (((0,), (0,)), ((), ())), preferred_element_type=F32)


def product(left, right):
    return jnp.dot(left, right, preferred_element_type=F32)


def head_scores(query, keys, allowed):
    scores = contract_last(query, keys) * (HD ** (-0.5))
    scores = jnp.where(allowed, scores, -1e30)
    weights_exp = jnp.exp(scores - jnp.max(scores, axis=-1, keepdims=True))
    return weights_exp, 1.0 / jnp.sum(weights_exp, axis=-1, keepdims=True)


def attend_forward_kernel(
    query_lin, keys, values, cosine, signed_sine, query_pos, key_pos, query_rot, mixed
):
    allowed = key_pos[...] <= query_pos[...]
    for head in range(HEADS_STEP):
        columns = slice(head * HD, (head + 1) * HD)
        linear = query_lin[:, columns]
        rotated = linear * cosine[...] + pltpu.roll(linear, HD // 2, 1) * signed_sine[...]
        rotated = rotated.astype(BF)
        query_rot[:, columns] = rotated
        weights_exp, inverse_sum = head_scores(rotated, keys[...], allowed)
        probabilities = (weights_exp * inverse_sum).astype(BF)
        mixed[:, columns] = product(probabilities, values[...]).astype(BF)


def attend_forward(query_lin, keys_values, cosine, signed_sine, query_pos, key_pos):
    rows, width = query_lin.shape
    count_all = keys_values.shape[0]
    per_kv = H // KVH // HEADS_STEP
    wide = HEADS_STEP * HD
    table = pl.BlockSpec((rows, HD), lambda step: (0, 0))
    by_head = pl.BlockSpec((rows, wide), lambda step: (0, step))
    return pl.pallas_call(
        attend_forward_kernel,
        grid=(H // HEADS_STEP,),
        in_specs=[
            by_head,
            pl.BlockSpec((count_all, HD), lambda step: (0, step // per_kv)),
            pl.BlockSpec((count_all, HD), lambda step: (0, KVH + step // per_kv)),
            table,
            table,
            pl.BlockSpec((rows, 1), lambda step: (0, 0)),
            pl.BlockSpec((1, count_all), lambda step: (0, 0)),
        ],
        out_specs=[by_head, by_head],
        out_shape=[jax.ShapeDtypeStruct((rows, width), BF)] * 2,
        compiler_params=pltpu.CompilerParams(vmem_limit_bytes=48 * 1024 * 1024),
        cost_estimate=pl.CostEstimate(
            flops=4 * rows * count_all * width,
            bytes_accessed=8 * rows * width + 2 * keys_values.size,
            transcendentals=H * rows * count_all,
        ),
    )(query_lin, keys_values, keys_values, cosine, signed_sine, query_pos, key_pos)


def attend_backward_kernel(
    query_rot,
    out_grad,
    keys,
    values,
    cosine,
    signed_sine,
    query_pos,
    key_pos,
    query_grad,
    key_grad,
    value_grad,
    key_sum,
    value_sum,
    *,
    per_kv,
):
    step = pl.program_id(0)
    allowed = key_pos[...] <= query_pos[...]
    scaling = HD ** (-0.5)

    @pl.when(step % per_kv == 0)
    def _():
        key_sum[...] = jnp.zeros_like(key_sum)
        value_sum[...] = jnp.zeros_like(value_sum)

    for head in range(HEADS_STEP):
        columns = slice(head * HD, (head + 1) * HD)
        query = query_rot[:, columns]
        grad = out_grad[:, columns]
        weights_exp, inverse_sum = head_scores(query, keys[...], allowed)
        probabilities = weights_exp * inverse_sum
        prob_grad = contract_last(grad, values[...])
        weighted = jnp.sum(probabilities * prob_grad, axis=-1, keepdims=True)
        score_grad = (probabilities * (prob_grad - weighted)).astype(BF)
        turned = product(score_grad, keys[...]) * scaling
        turned = turned * cosine[...] - pltpu.roll(turned, HD // 2, 1) * signed_sine[...]
        query_grad[:, columns] = turned.astype(BF)
        key_sum[...] += contract_first(score_grad, query) * scaling
        value_sum[...] += contract_first(probabilities.astype(BF), grad)

    @pl.when(step % per_kv == per_kv - 1)
    def _():
        key_grad[...] = key_sum[...].astype(BF)
        value_grad[...] = value_sum[...].astype(BF)


def attend_backward(query_rot, out_grad, keys_values, cosine, signed_sine, query_pos, key_pos):
    rows, width = query_rot.shape
    count_all = keys_values.shape[0]
    per_kv = H // KVH // HEADS_STEP
    wide = HEADS_STEP * HD
    table = pl.BlockSpec((rows, HD), lambda step: (0, 0))
    by_head = pl.BlockSpec((rows, wide), lambda step: (0, step))
    by_kv = pl.BlockSpec((count_all, HD), lambda step: (0, step // per_kv))
    return pl.pallas_call(
        functools.partial(attend_backward_kernel, per_kv=per_kv),
        grid=(H // HEADS_STEP,),
        in_specs=[
            by_head,
            by_head,
            by_kv,
            pl.BlockSpec((count_all, HD), lambda step: (0, KVH + step // per_kv)),
            table,
            table,
            pl.BlockSpec((rows, 1), lambda step: (0, 0)),
            pl.BlockSpec((1, count_all), lambda step: (0, 0)),
        ],
        out_specs=[by_head, by_kv, by_kv],
        out_shape=[
            jax.ShapeDtypeStruct((rows, width), BF),
            jax.ShapeDtypeStruct((count_all, KVH * HD), BF),
            jax.ShapeDtypeStruct((count_all, KVH * HD), BF),
        ],
        scratch_shapes=[pltpu.VMEM((count_all, HD), F32)] * 2,
        compiler_params=pltpu.CompilerParams(vmem_limit_bytes=48 * 1024 * 1024),
        cost_estimate=pl.CostEstimate(
            flops=10 * rows * count_all * width,
            bytes_accessed=8 * rows * width + 4 * keys_values.size,
            transcendentals=H * rows * count_all,
        ),
    )(query_rot, out_grad, keys_values, keys_values, cosine, signed_sine, query_pos, key_pos)


def swap_fsdp(values, mask):
    count = lax.axis_size("fsdp")
    return lax.ppermute(values, "fsdp", [(i, i ^ mask) for i in range(count)])


def gather_tokens(rows):
    if lax.axis_size("fsdp") != 8:
        return lax.all_gather(rows, "fsdp", axis=0, tiled=True)
    half = rows.shape[0] // 2
    from_x = swap_fsdp(rows, 2)
    from_y = swap_fsdp(rows, 4)
    far_first = swap_fsdp(from_y[:half], 2)
    far_last = swap_fsdp(from_x[half:], 4)
    own_core = jnp.concatenate([rows, from_x, from_y, far_first, far_last], axis=0)
    return jnp.concatenate([own_core, swap_fsdp(own_core, 1)], axis=0)


def scatter_tokens(partial):
    count = lax.axis_size("fsdp")
    if count != 8:
        return lax.psum_scatter(partial, "fsdp", scatter_dimension=0, tiled=True).astype(F32)
    rows = partial.shape[0] // count
    half = rows // 2
    other = swap_fsdp(partial[4 * rows :], 1)
    summed = (partial[: 4 * rows].astype(F32) + other.astype(F32)).astype(BF)
    own, to_x, to_y, far = (summed[k * rows : (k + 1) * rows] for k in range(4))
    by_x = swap_fsdp(far[:half], 2)
    by_y = swap_fsdp(far[half:], 4)
    to_y = jnp.concatenate([(to_y[:half].astype(F32) + by_x.astype(F32)).astype(BF), to_y[half:]], axis=0)
    to_x = jnp.concatenate([to_x[:half], (to_x[half:].astype(F32) + by_y.astype(F32)).astype(BF)], axis=0)
    return own.astype(F32) + swap_fsdp(to_x, 2).astype(F32) + swap_fsdp(to_y, 4).astype(F32)


def sp_reduce_scatter(take_part):
    count = lax.axis_size("sp")
    place = lax.axis_index("sp")
    up, down = None, None
    for step in range(1, count):
        part_up = take_part(jnp.clip(count - step + place, 0, count - 1))
        part_down = take_part(jnp.clip(step - count + place, 0, count - 1))
        if up is not None:
            part_up = (part_up.astype(F32) + up.astype(F32)).astype(BF)
            part_down = (part_down.astype(F32) + down.astype(F32)).astype(BF)
        up = lax.ppermute(part_up, "sp", [(i, i + 1) for i in range(step)])
        down = lax.ppermute(part_down, "sp", [(count - 1 - i, count - 2 - i) for i in range(step)])
    own = take_part(place)
    return (own.astype(F32) + up.astype(F32) + down.astype(F32)).astype(BF)


def sp_all_gather(own):
    count = lax.axis_size("sp")
    place = lax.axis_index("sp")
    up, down = own, own
    found = [own] * count
    for step in range(1, count):
        up = lax.ppermute(up, "sp", [(i, i + 1) for i in range(step - 1, count - 1)])
        down = lax.ppermute(down, "sp", [(count - 1 - i, count - 2 - i) for i in range(step - 1, count - 1)])
        for index in range(count):
            found[index] = jnp.where(place - index == step, up, found[index])
            found[index] = jnp.where(index - place == step, down, found[index])
    return found


def per_device(
    tokens,
    cotangent,
    seq_lengths,
    block_order,
    w_query,
    w_key,
    w_value,
    b_query,
    b_key,
    b_value,
    w_output,
    gain_attn,
    gain_mlp,
    w_gate,
    w_up,
    w_down,
):
    local_rows, width = tokens.shape
    sp_count = lax.axis_size("sp")
    sp_index = lax.axis_index("sp")
    fsdp_count = lax.axis_size("fsdp")
    fsdp_index = lax.axis_index("fsdp")
    group_rows = local_rows * sp_count
    block_rows = local_rows // 2
    query_width = H * HD
    key_width = KVH * HD
    hidden_all = w_gate.shape[1]
    hidden_width = hidden_all // fsdp_count
    shard_rows = w_gate.shape[0]

    w_kv = lax.all_gather(jnp.concatenate([w_key, w_value], axis=1), "fsdp", axis=0, tiled=True)
    vectors = lax.all_gather(
        jnp.concatenate([b_query, b_key, b_value, gain_attn, gain_mlp])[None, :], "fsdp", axis=0, tiled=True
    ).astype(F32)
    widths = [b_query.shape[0], b_key.shape[0], b_value.shape[0], gain_attn.shape[0], gain_mlp.shape[0]]
    edges = [sum(widths[:n]) for n in range(len(widths) + 1)]
    bias_q, bias_k, bias_v, gain_one, gain_two = (
        vectors[:, edges[n] : edges[n + 1]].reshape(-1) for n in range(len(widths))
    )
    w_q = lax.all_gather(w_query, "fsdp", axis=0, tiled=True)
    w_o = lax.all_gather(w_output, "fsdp", axis=0, tiled=True)

    gate_up = jnp.stack(
        [
            w_gate.reshape(shard_rows, fsdp_count, hidden_width),
            w_up.reshape(shard_rows, fsdp_count, hidden_width),
        ],
        axis=0,
    ).transpose(2, 0, 1, 3)
    gate_up = lax.all_to_all(gate_up, "fsdp", split_axis=0, concat_axis=0, tiled=True)
    my_gate = gate_up[:, 0].reshape(width, hidden_width)
    my_up = gate_up[:, 1].reshape(width, hidden_width)

    order_row = block_order[0]
    local_pos = stream_positions(order_row, sp_index * local_rows, local_rows, block_rows)
    group_pos = stream_positions(order_row, 0, group_rows, block_rows)
    query_pos, key_pos = local_pos[:, None], group_pos[None, :]
    valid_rows = (local_pos < seq_lengths[0]).astype(F32)[:, None]
    upstream = cotangent.astype(F32)
    mlp_grad = gather_tokens((valid_rows * upstream).astype(BF))

    inputs = tokens.astype(F32)
    scale_one = lax.rsqrt(jnp.mean(inputs * inputs, axis=-1, keepdims=True) + EPS)
    unit_one = inputs * scale_one
    normed_one = (unit_one * gain_one).astype(BF)
    cosine, signed_sine = rotary_tables(local_pos)
    kv_lin = product(normed_one, w_kv)
    key_lin = (kv_lin[:, :key_width] + bias_k).reshape(local_rows, KVH, HD)
    key_rot = key_lin * cosine[:, None, :] + swap_halves(key_lin) * signed_sine[:, None, :]
    keys_values = jnp.concatenate(
        [key_rot.reshape(local_rows, key_width).astype(BF), (kv_lin[:, key_width:] + bias_v).astype(BF)], axis=1
    )
    keys_values = lax.all_gather(keys_values, "sp", axis=0, tiled=True)
    query_lin = product(normed_one, w_q) + bias_q
    query_rot, mixed = attend_forward(query_lin, keys_values, cosine, signed_sine, query_pos, key_pos)
    attn_branch = product(mixed, w_o)
    hidden_in = inputs + valid_rows * attn_branch
    scale_two = lax.rsqrt(jnp.mean(hidden_in * hidden_in, axis=-1, keepdims=True) + EPS)
    unit_two = hidden_in * scale_two
    normed_two = gather_tokens((unit_two * gain_two).astype(BF))

    gate_lin = product(normed_two, my_gate)
    up_lin = product(normed_two, my_up)
    hidden_grad = contract_last(mlp_grad, w_down)
    sigma = jax.nn.sigmoid(gate_lin)
    activated = gate_lin * sigma
    hidden = (activated * up_lin).astype(BF)
    gate_grad = (hidden_grad * up_lin * (sigma * (1.0 + gate_lin * (1.0 - sigma)))).astype(BF)
    up_grad = (hidden_grad * activated).astype(BF)
    normed_two_grad = scatter_tokens((contract_last(gate_grad, my_gate) + contract_last(up_grad, my_up)).astype(BF))
    mlp_branch = scatter_tokens(product(hidden, w_down).astype(BF))

    sp_rows = shard_rows // sp_count

    def down_part(index):
        part = hidden_width // sp_count
        return lax.dynamic_slice_in_dim(down_term, index * part, part, 0)

    def split_rows(term):
        blocks = term.reshape(fsdp_count, sp_count, sp_rows, hidden_width)
        return lambda index: lax.dynamic_index_in_dim(blocks, index, 1, keepdims=False)

    def gather_rows(own):
        own = lax.all_to_all(own, "fsdp", split_axis=0, concat_axis=0, tiled=True)
        parts = [part.transpose(1, 0, 2).reshape(sp_rows, hidden_all) for part in sp_all_gather(own)]
        return jnp.concatenate(parts, axis=0).astype(F32)

    down_term = contract_first(hidden, mlp_grad).astype(BF)
    grad_down = jnp.concatenate(sp_all_gather(sp_reduce_scatter(down_part)), axis=0).astype(F32)
    gate_term = contract_first(normed_two, gate_grad).astype(BF)
    grad_gate = gather_rows(sp_reduce_scatter(split_rows(gate_term)))
    up_term = contract_first(normed_two, up_grad).astype(BF)
    grad_up = gather_rows(sp_reduce_scatter(split_rows(up_term)))

    result = hidden_in + valid_rows * mlp_branch
    gain_two_grad, norm_two_back = norm_backward(normed_two_grad, unit_two, gain_two, scale_two)
    hidden_in_grad = upstream + norm_two_back
    attn_grad = (valid_rows * hidden_in_grad).astype(BF)
    mixed_grad = contract_last(attn_grad, w_o).astype(BF)
    query_lin_grad, key_part, value_part = attend_backward(
        query_rot, mixed_grad, keys_values, cosine, signed_sine, query_pos, key_pos
    )
    pair_total = lax.psum_scatter(
        jnp.concatenate([key_part, value_part], axis=1), "sp", scatter_dimension=0, tiled=True
    ).astype(F32)
    key_rot_grad = pair_total[:, :key_width].reshape(local_rows, KVH, HD)
    key_lin_grad = key_rot_grad * cosine[:, None, :] - swap_halves(key_rot_grad) * signed_sine[:, None, :]
    kv_lin_grad = jnp.concatenate(
        [key_lin_grad.reshape(local_rows, key_width).astype(BF), pair_total[:, key_width:].astype(BF)], axis=1
    )
    normed_one_grad = contract_last(query_lin_grad, w_q) + contract_last(kv_lin_grad, w_kv)
    gain_one_grad, norm_one_back = norm_backward(normed_one_grad, unit_one, gain_one, scale_one)
    input_grad = hidden_in_grad + norm_one_back

    output_term = contract_first(mixed, attn_grad).astype(BF)
    output_share = lax.psum_scatter(output_term, "fsdp", scatter_dimension=0, tiled=True)
    projection_term = contract_first(normed_one, jnp.concatenate([query_lin_grad, kv_lin_grad], axis=1)).astype(BF)
    projection_share = lax.psum_scatter(projection_term, "fsdp", scatter_dimension=0, tiled=True)
    attn_share = jnp.concatenate([projection_share, output_share], axis=1)

    def attn_part(index):
        return lax.dynamic_slice_in_dim(attn_share, index * sp_rows, sp_rows, 0)

    attn_full = jnp.concatenate(sp_all_gather(sp_reduce_scatter(attn_part)), axis=0).astype(F32)

    stat_parts = jnp.stack(
        [
            jnp.sum(valid_rows * result * result),
            jnp.sum(valid_rows * attn_branch * attn_branch),
            jnp.sum(valid_rows * mlp_branch * mlp_branch),
            jnp.sum(valid_rows),
        ]
    )
    summed = lax.psum(
        (
            jnp.sum(query_lin_grad.astype(F32), axis=0),
            jnp.sum(kv_lin_grad.astype(F32), axis=0),
            gain_one_grad,
            gain_two_grad,
            stat_parts,
        ),
        ("fsdp", "sp"),
    )

    def own_piece(vector):
        width_piece = vector.shape[0] // fsdp_count
        return lax.dynamic_slice_in_dim(vector, fsdp_index * width_piece, width_piece, 0)

    totals = summed[4]
    root_means = jnp.sqrt(totals[:3] / (totals[3] * width))
    return (
        result.astype(BF),
        input_grad,
        attn_full[:, :query_width],
        attn_full[:, query_width : query_width + key_width],
        attn_full[:, query_width + key_width : query_width + 2 * key_width],
        own_piece(summed[0]),
        own_piece(summed[1][:key_width]),
        own_piece(summed[1][key_width:]),
        attn_full[:, query_width + 2 * key_width :],
        own_piece(summed[2]),
        own_piece(summed[3]),
        grad_gate,
        grad_up,
        grad_down,
        root_means,
    )


def solution(mesh):
    both, first = P(("fsdp", "sp"), None), P("fsdp", None)
    one = P("fsdp")
    in_specs = (both, both, one, first, first, first, first, one, one, one, first, one, one, first, first, first)
    out_specs = (both, both, first, first, first, one, one, one, first, one, one, first, first, first, P())
    return jax.shard_map(per_device, mesh=mesh, in_specs=in_specs, out_specs=out_specs, check_vma=False)
```

```python
import functools

import jax
import jax.numpy as jnp
from jax import lax
from jax.experimental import pallas as pl
from jax.experimental.pallas import tpu as pltpu
from jax.sharding import PartitionSpec as P

H = 12
KVH = 2
HD = 128
HEADS_STEP = 2
LANES = 128


EPS = 1e-06
THETA = 1000000.0
BF = jnp.bfloat16
F32 = jnp.float32


def rotary_tables(positions):
    half_width = HD // 2
    inverse = THETA ** (-(jnp.arange(half_width, dtype=F32) * 2.0) / HD)
    angles = positions.astype(F32)[:, None] * inverse[None, :]
    cosine, sine = jnp.cos(angles), jnp.sin(angles)
    return (
        jnp.concatenate([cosine, cosine], axis=-1),
        jnp.concatenate([-sine, sine], axis=-1),
    )


def swap_halves(values):
    half_width = HD // 2
    return jnp.concatenate([values[..., half_width:], values[..., :half_width]], axis=-1)


def stream_positions(order_row, first_row, row_count, block_size):
    row_ids = first_row + jnp.arange(row_count, dtype=jnp.int32)
    which_block = row_ids // block_size
    matches = jnp.arange(order_row.shape[0], dtype=jnp.int32)[None, :] == which_block[:, None]
    block_start = jnp.sum(jnp.where(matches, order_row[None, :], 0), axis=1)
    return block_start * block_size + row_ids % block_size


def norm_backward(normed_grad, unit_rows, gain_rows, scale_rows):
    gain_grad = jnp.sum(normed_grad * unit_rows, axis=0)
    scaled = normed_grad * gain_rows
    inner = jnp.mean(scaled * unit_rows, axis=-1, keepdims=True)
    return (gain_grad, scale_rows * (scaled - unit_rows * inner))


def contract_last(left, right):
    return lax.dot_general(left, right, (((1,), (1,)), ((), ())), preferred_element_type=F32)


def contract_first(left, right):
    return lax.dot_general(left, right, (((0,), (0,)), ((), ())), preferred_element_type=F32)


def product(left, right):
    return jnp.dot(left, right, preferred_element_type=F32)


def head_scores(query, keys, allowed):
    scores = contract_last(query, keys) * (HD ** (-0.5))
    scores = jnp.where(allowed, scores, -1e30)
    weights_exp = jnp.exp(scores - jnp.max(scores, axis=-1, keepdims=True))
    return weights_exp, 1.0 / jnp.sum(weights_exp, axis=-1, keepdims=True)


def attend_forward_kernel(
    query_lin, keys, values, cosine, signed_sine, query_pos, key_pos, query_rot, mixed
):
    allowed = key_pos[...] <= query_pos[...]
    for head in range(HEADS_STEP):
        columns = slice(head * HD, (head + 1) * HD)
        linear = query_lin[:, columns]
        rotated = linear * cosine[...] + pltpu.roll(linear, HD // 2, 1) * signed_sine[...]
        rotated = rotated.astype(BF)
        query_rot[:, columns] = rotated
        weights_exp, inverse_sum = head_scores(rotated, keys[...], allowed)
        probabilities = (weights_exp * inverse_sum).astype(BF)
        mixed[:, columns] = product(probabilities, values[...]).astype(BF)


def attend_forward(query_lin, keys_values, cosine, signed_sine, query_pos, key_pos):
    rows, width = query_lin.shape
    count_all = keys_values.shape[0]
    per_kv = H // KVH // HEADS_STEP
    wide = HEADS_STEP * HD
    table = pl.BlockSpec((rows, HD), lambda step: (0, 0))
    by_head = pl.BlockSpec((rows, wide), lambda step: (0, step))
    return pl.pallas_call(
        attend_forward_kernel,
        grid=(H // HEADS_STEP,),
        in_specs=[
            by_head,
            pl.BlockSpec((count_all, HD), lambda step: (0, step // per_kv)),
            pl.BlockSpec((count_all, HD), lambda step: (0, KVH + step // per_kv)),
            table,
            table,
            pl.BlockSpec((rows, 1), lambda step: (0, 0)),
            pl.BlockSpec((1, count_all), lambda step: (0, 0)),
        ],
        out_specs=[by_head, by_head],
        out_shape=[jax.ShapeDtypeStruct((rows, width), BF)] * 2,
        compiler_params=pltpu.CompilerParams(vmem_limit_bytes=48 * 1024 * 1024),
        cost_estimate=pl.CostEstimate(
            flops=4 * rows * count_all * width,
            bytes_accessed=8 * rows * width + 2 * keys_values.size,
            transcendentals=H * rows * count_all,
        ),
    )(query_lin, keys_values, keys_values, cosine, signed_sine, query_pos, key_pos)


def attend_backward_kernel(
    query_rot, out_grad, keys, values, cosine, signed_sine, query_pos, key_pos, query_grad, pair_grad, key_sum, value_sum
):
    step = pl.program_id(0)
    allowed = key_pos[...] <= query_pos[...]
    scaling = HD ** (-0.5)

    @pl.when(step == 0)
    def _():
        key_sum[...] = jnp.zeros_like(key_sum)
        value_sum[...] = jnp.zeros_like(value_sum)

    for head in range(HEADS_STEP):
        columns = slice(head * HD, (head + 1) * HD)
        query = query_rot[:, columns]
        grad = out_grad[:, columns]
        weights_exp, inverse_sum = head_scores(query, keys[...], allowed)
        probabilities = weights_exp * inverse_sum
        prob_grad = contract_last(grad, values[...])
        weighted = jnp.sum(probabilities * prob_grad, axis=-1, keepdims=True)
        score_grad = (probabilities * (prob_grad - weighted)).astype(BF)
        turned = product(score_grad, keys[...]) * scaling
        turned = turned * cosine[...] - pltpu.roll(turned, HD // 2, 1) * signed_sine[...]
        query_grad[:, columns] = turned.astype(BF)
        key_sum[...] += contract_first(score_grad, query) * scaling
        value_sum[...] += contract_first(probabilities.astype(BF), grad)

    @pl.when(step == pl.num_programs(0) - 1)
    def _():
        pair_grad[:, :HD] = key_sum[...].astype(BF)
        pair_grad[:, HD:] = value_sum[...].astype(BF)


def attend_backward(earlier, number, query_rot, out_grad, keys_values, cosine, signed_sine, query_pos, key_pos):
    rows = query_rot.shape[0]
    count_all = keys_values.shape[0]
    per_kv = H // KVH // HEADS_STEP
    wide = HEADS_STEP * HD
    table = pl.BlockSpec((rows, HD), lambda step: (0, 0))
    by_head = pl.BlockSpec((rows, wide), lambda step: (0, number * per_kv + step))
    in_specs = [
        by_head,
        by_head,
        pl.BlockSpec((count_all, HD), lambda step: (0, number)),
        pl.BlockSpec((count_all, HD), lambda step: (0, KVH + number)),
        table,
        table,
        pl.BlockSpec((rows, 1), lambda step: (0, 0)),
        pl.BlockSpec((1, count_all), lambda step: (0, 0)),
    ]
    out_specs = [
        pl.BlockSpec((rows, wide), lambda step: (0, step)),
        pl.BlockSpec((count_all, 2 * HD), lambda step: (0, 0)),
    ]
    out_shape = [
        jax.ShapeDtypeStruct((rows, per_kv * wide), BF),
        jax.ShapeDtypeStruct((count_all, 2 * HD), BF),
    ]
    operands = (query_rot, out_grad, keys_values, keys_values, cosine, signed_sine, query_pos, key_pos)
    scratch = [pltpu.VMEM((count_all, HD), F32)] * 2
    call = ordered_call(
        attend_backward_kernel, operands, in_specs, out_specs, out_shape, earlier, (per_kv,), scratch=scratch, vmem=48
    )
    return call(*operands, *earlier)


def chunk_widths(hidden_width):
    first = max(LANES, hidden_width // (2 * LANES) * LANES)
    return [first, hidden_width - first]


def round_up(value, step):
    return (value + step - 1) // step * step


def cut_kernel(gate, up, *outputs, hidden_width, widths):
    count = gate.shape[1] // hidden_width
    for owner in range(count):
        column = owner * hidden_width
        for out, wide in zip(outputs, widths):
            padded = round_up(wide, LANES)
            first = column // LANES * LANES
            shift = column - first
            span = round_up(shift + wide, LANES)
            for half, source in enumerate((gate, up)):
                part = source[:, first : first + span].astype(F32)
                if shift:
                    part = pltpu.roll(part, span - shift, 1)
                if span < padded:
                    part = jnp.concatenate([part, jnp.zeros((part.shape[0], padded - span), F32)], axis=1)
                part = part[:, :padded]
                if wide < padded:
                    lane = lax.broadcasted_iota(jnp.int32, part.shape, 1)
                    part = jnp.where(lane < wide, part, 0.0)
                out[owner, :, half * padded : (half + 1) * padded] = part.astype(BF)
            column += wide


def cut_gate_up(w_gate, w_up, hidden_width, widths):
    rows, total = w_gate.shape
    count = total // hidden_width
    return pl.pallas_call(
        functools.partial(cut_kernel, hidden_width=hidden_width, widths=widths),
        out_shape=[jax.ShapeDtypeStruct((count, rows, 2 * round_up(wide, LANES)), BF) for wide in widths],
        compiler_params=pltpu.CompilerParams(vmem_limit_bytes=48 * 1024 * 1024),
        cost_estimate=pl.CostEstimate(flops=4 * w_gate.size, bytes_accessed=8 * w_gate.size, transcendentals=0),
    )(w_gate, w_up)


def swap_fsdp(values, mask):
    count = lax.axis_size("fsdp")
    return lax.ppermute(values, "fsdp", [(i, i ^ mask) for i in range(count)])


def after(value, *others):
    return lax.optimization_barrier((value,) + others)[0]


def place_kernel(index, *refs, sizes):
    count = len(sizes)
    pieces, out, semaphores = refs[:count], refs[count], refs[count + 1]
    copies = []
    for number, (mask, first, size) in enumerate(sizes):
        start = jnp.bitwise_xor(index[0], mask) * (out.shape[0] // 8) + first
        target = out.at[pl.ds(pl.multiple_of(start, 16), size)]
        copies.append(pltpu.make_async_copy(pieces[number], target, semaphores.at[number]))
        copies[-1].start()
    for copy in copies:
        copy.wait()


def place_parts(parts, index):
    rows = sum(part.shape[0] for _, _, part in parts)
    columns, dtype = parts[0][2].shape[1], parts[0][2].dtype
    sizes = [(mask, first, part.shape[0]) for mask, first, part in parts]
    anywhere = pl.BlockSpec(memory_space=pl.ANY)
    return pl.pallas_call(
        functools.partial(place_kernel, sizes=sizes),
        in_specs=[pl.BlockSpec(memory_space=pltpu.SMEM)] + [anywhere] * len(parts),
        out_specs=pl.BlockSpec(memory_space=pltpu.VMEM),
        out_shape=jax.ShapeDtypeStruct((rows, columns), dtype),
        scratch_shapes=[pltpu.SemaphoreType.DMA((len(parts),))],
        compiler_params=pltpu.CompilerParams(vmem_limit_bytes=32 * 1024 * 1024),
        cost_estimate=pl.CostEstimate(flops=0, bytes_accessed=4 * rows * columns, transcendentals=0),
    )(index, *(part for _, _, part in parts))


def gather_rows(rows, index, *earlier):
    if lax.axis_size("fsdp") != 8:
        return lax.all_gather(rows, "fsdp", axis=0, tiled=True), (rows,), (rows,)
    size = rows.shape[0]
    half = size // 2
    rows = after(rows, *earlier)
    from_x = swap_fsdp(rows, 2)
    from_y = swap_fsdp(rows, 4)
    far_first = swap_fsdp(from_y[:half], 2)
    far_last = swap_fsdp(from_x[half:], 4)
    parts = []
    for mask, first, part in ((0, 0, rows), (2, 0, from_x), (4, 0, from_y), (6, 0, far_first), (6, half, far_last)):
        parts.append((mask, first, part))
        parts.append((mask ^ 1, first, swap_fsdp(part, 1)))
    return place_parts(parts, index), (from_x, from_y), (far_first, far_last)


def gather_small(rows, index):
    if lax.axis_size("fsdp") != 8:
        return lax.all_gather(rows, "fsdp", axis=0, tiled=True), (rows,)
    found = [(mask, rows if mask == 0 else swap_fsdp(rows, mask)) for mask in (0, 2, 4, 6)]
    parts = [(mask, 0, part) for mask, part in found]
    parts += [(mask ^ 1, 0, swap_fsdp(part, 1)) for mask, part in found]
    return place_parts(parts, index), tuple(part for _, part in found)


COVER = 10**12


def ordered_call(kernel, operands, in_specs, out_specs, out_shape, earlier, grid=(), scalars=0, scratch=(), vmem=16):
    count = scalars + len(operands)

    def body(*refs):
        kernel(*refs[:count], *refs[count + len(earlier) :])

    return pl.pallas_call(
        body,
        grid_spec=pltpu.PrefetchScalarGridSpec(
            num_scalar_prefetch=scalars,
            grid=grid,
            in_specs=list(in_specs) + [pl.BlockSpec(memory_space=pl.ANY)] * len(earlier),
            out_specs=out_specs,
            scratch_shapes=scratch,
        ),
        out_shape=out_shape,
        compiler_params=pltpu.CompilerParams(vmem_limit_bytes=vmem * 1024 * 1024),
        cost_estimate=pl.CostEstimate(flops=COVER, bytes_accessed=1024, transcendentals=0),
    )


def spacer_kernel(out):
    out[...] = jnp.zeros_like(out)


def spacer(earlier):
    out_shape = jax.ShapeDtypeStruct((8, LANES), F32)
    return ordered_call(spacer_kernel, (), [], pl.BlockSpec(memory_space=pltpu.VMEM), out_shape, earlier)(*earlier)


class Line:
    def __init__(self, ready):
        self.ready = ready
        self.marks = []
        self.last = ()

    def kernel(self, call, *arrived):
        found = call(self.last + arrived)
        self.last = (jax.tree.leaves(found)[0],)
        return found

    def step(self, work, *arrived):
        ready = self.ready
        arrived = self.last + arrived

        def marked():
            return work(), [array[(0,) * (array.ndim - 1)][:1] for array in arrived]

        shapes = jax.eval_shape(marked)

        def skip():
            return jnp.logical_not(ready), jax.tree.map(lambda leaf: jnp.zeros(leaf.shape, leaf.dtype), shapes)

        self.ready, (found, marks) = lax.cond(ready, lambda: (ready, marked()), skip)
        self.marks += marks
        self.last = (jax.tree.leaves(found)[0],)
        self.kernel(spacer)
        return found


def add_kernel(left, right, out):
    out[...] = (left[...].astype(F32) + right[...].astype(F32)).astype(BF)


def add_low(earlier, left, right):
    shape = left.shape
    columns = shape[-1]
    left, right = left.reshape(-1, columns), right.reshape(-1, columns)
    total = left.shape[0]
    rows = next(size for size in (768, 512, 384, 256, 192, 128, 64, 32, 16, total) if total % size == 0)
    block = pl.BlockSpec((rows, columns), lambda step: (step, 0))
    out_shape = jax.ShapeDtypeStruct(left.shape, BF)
    call = ordered_call(add_kernel, (left, right), [block] * 2, block, out_shape, earlier, (total // rows,), vmem=32)
    return call(left, right, *earlier).reshape(shape)


def split_kernel(same, other, own, to_x, to_y, far_first, far_last):
    rows = own.shape[0]
    half = rows // 2
    for first, out in ((0, own), (rows, to_x), (2 * rows, to_y), (3 * rows, far_first), (3 * rows + half, far_last)):
        size = out.shape[0]
        left, right = same[first : first + size], other[first : first + size]
        out[...] = (left.astype(F32) + right.astype(F32)).astype(BF)


def far_masks(other):
    return (1, 3, 5, 7) if other else (0, 2, 4, 6)


def pick_shards(partial, other):
    if partial.shape[0] != 8:
        return partial.reshape(-1, partial.shape[2])
    index = lax.axis_index("fsdp")
    parts = [lax.dynamic_index_in_dim(partial, index ^ mask, 0, keepdims=False) for mask in far_masks(other)]
    return jnp.concatenate(parts, axis=0)


def from_core(other):
    return swap_fsdp(other, 1) if lax.axis_size("fsdp") == 8 else other


def split_sum(earlier, same, moved):
    if lax.axis_size("fsdp") != 8:
        return [lax.psum_scatter(same, "fsdp", scatter_dimension=0, tiled=True)]
    rows, columns = same.shape[0] // 4, same.shape[1]
    sizes = (rows, rows, rows, rows // 2, rows // 2)
    whole = pl.BlockSpec(memory_space=pltpu.VMEM)
    out_shape = [jax.ShapeDtypeStruct((size, columns), BF) for size in sizes]
    call = ordered_call(split_kernel, (same, moved), [whole] * 2, [whole] * 5, out_shape, earlier, vmem=32)
    return call(same, moved, *earlier)


def from_far(begun):
    return [swap_fsdp(begun[3], 2), swap_fsdp(begun[4], 4)] if len(begun) == 5 else begun


def mix_kernel(to_x, to_y, by_x, by_y, out_x, out_y):
    half = by_x.shape[0]
    out_x[:half] = to_x[:half]
    out_x[half:] = (to_x[half:].astype(F32) + by_y[...].astype(F32)).astype(BF)
    out_y[:half] = (to_y[:half].astype(F32) + by_x[...].astype(F32)).astype(BF)
    out_y[half:] = to_y[half:]


def mix_sum(earlier, begun, moved):
    if len(begun) != 5:
        return begun
    own, to_x, to_y = begun[:3]
    whole = pl.BlockSpec(memory_space=pltpu.VMEM)
    out_shape = [jax.ShapeDtypeStruct(to_x.shape, BF)] * 2
    operands = (to_x, to_y, *moved)
    call = ordered_call(mix_kernel, operands, [whole] * 4, [whole] * 2, out_shape, earlier, vmem=32)
    return [own] + list(call(*operands, *earlier))


def from_near(sent):
    return [sent[0], swap_fsdp(sent[1], 2), swap_fsdp(sent[2], 4)] if len(sent) == 3 else sent


def sum_kernel(*refs):
    total = refs[0][...].astype(F32)
    for part in refs[1:-1]:
        total = total + part[...].astype(F32)
    refs[-1][...] = total.astype(BF)


def sum_low(earlier, parts):
    whole = pl.BlockSpec(memory_space=pltpu.VMEM)
    out_shape = jax.ShapeDtypeStruct(parts[0].shape, BF)
    call = ordered_call(sum_kernel, tuple(parts), [whole] * len(parts), whole, out_shape, earlier, vmem=32)
    return call(*parts, *earlier)


def sum_parts(parts):
    total = parts[0].astype(F32)
    for part in parts[1:]:
        total = total + part.astype(F32)
    return total


def to_middle(values):
    return lax.ppermute(values, "sp", [(0, 1), (3, 2)])


def across_middle(values):
    return lax.ppermute(values, "sp", [(1, 2), (2, 1)])


def to_ends(values):
    return lax.ppermute(values, "sp", [(1, 0), (2, 3)])


def pick_sum(total, moved):
    place = lax.axis_index("sp")
    return jnp.where((place == 1) | (place == 2), total, moved)


def join_kernel(middle, *refs, hidden_width, widths):
    out = refs[-1]
    chunks = [refs[2 * n : 2 * n + 2] for n in range(len(widths))]
    total = out.shape[1]

    def fill(number):
        for owner in range(total // hidden_width):
            column = owner * hidden_width
            for chunk, wide in zip(chunks, widths):
                part = chunk[number][owner].astype(F32)
                first = column // LANES * LANES
                shift = column - first
                span = round_up(shift + wide, LANES)
                if span > part.shape[1]:
                    part = jnp.concatenate([part, jnp.zeros((part.shape[0], span - part.shape[1]), F32)], axis=1)
                if shift:
                    part = pltpu.roll(part, shift, 1)
                    lane = lax.broadcasted_iota(jnp.int32, (part.shape[0], LANES), 1)
                    head = jnp.where(lane >= shift, part[:, :LANES], out[:, first : first + LANES])
                    out[:, first : first + LANES] = head
                    if span > LANES:
                        out[:, first + LANES : first + span] = part[:, LANES:span]
                else:
                    out[:, first : first + span] = part[:, :span]
                column += wide

    @pl.when(middle[0] == 1)
    def _():
        fill(0)

    @pl.when(middle[0] == 0)
    def _():
        fill(1)


def join_columns(earlier, found, columns, hidden_width, widths):
    place = lax.axis_index("sp")
    middle = ((place == 1) | (place == 2)).astype(jnp.int32)[None]
    arrays = [part for chunk in found for part in chunk]
    count, total = arrays[0].shape[:2]
    rows = 16
    in_specs = [pl.BlockSpec(memory_space=pltpu.SMEM)]
    for wide, column in zip(widths, columns):
        block = pl.BlockSpec((count, rows, round_up(wide, LANES)), lambda block, column=column: (0, block, column))
        in_specs += [block, block]
    out_specs = pl.BlockSpec((rows, count * hidden_width), lambda block: (block, 0))
    out_shape = jax.ShapeDtypeStruct((total, count * hidden_width), F32)
    operands = (middle, *arrays)
    kernel = functools.partial(join_kernel, hidden_width=hidden_width, widths=widths)
    call = ordered_call(kernel, operands, in_specs, out_specs, out_shape, earlier, (total // rows,), vmem=32)
    return call(*operands, *earlier)


def activate_kernel(normed, grad, weights, down, hidden_out, grads_out, *, first):
    padded = weights.shape[1] // 2
    rows = normed[...]
    gate = product(rows, weights[:, :padded])
    up = product(rows, weights[:, padded:])
    hidden_grad = contract_last(grad[...], down[first : first + padded])
    sigma = 1.0 / (1.0 + jnp.exp(-gate))
    activated = gate * sigma
    hidden_out[...] = (activated * up).astype(BF)
    grads_out[:, :padded] = (hidden_grad * up * (sigma * (1.0 + gate * (1.0 - sigma)))).astype(BF)
    grads_out[:, padded:] = (hidden_grad * activated).astype(BF)


def activate(earlier, normed, grad, weights, down, first):
    total, width = normed.shape
    wide = weights.shape[1] // 2
    rows = 256
    by_rows = pl.BlockSpec((rows, width), lambda step: (step, 0))
    in_specs = [
        by_rows,
        by_rows,
        pl.BlockSpec(weights.shape, lambda step: (0, 0)),
        pl.BlockSpec(down.shape, lambda step: (0, 0)),
    ]
    out_specs = [pl.BlockSpec((rows, wide * n), lambda step: (step, 0)) for n in (1, 2)]
    out_shape = [jax.ShapeDtypeStruct((total, wide * n), BF) for n in (1, 2)]
    operands = (normed, grad, weights, down)
    kernel = functools.partial(activate_kernel, first=first)
    call = ordered_call(kernel, operands, in_specs, out_specs, out_shape, earlier, (total // rows,), vmem=56)
    return call(*operands, *earlier)


def back_kernel(order, grads_1, grads_2, weights_1, weights_2, out):
    total = contract_last(grads_1[...], weights_1[...]) + contract_last(grads_2[...], weights_2[...])
    out[...] = total.astype(BF)


def branch_kernel(order, hidden_1, hidden_2, down, out):
    first = hidden_1.shape[1]
    total = product(hidden_1[...], down[:first]) + product(hidden_2[...], down[first:])
    out[...] = total.astype(BF)


def row_products(earlier, kernel, lefts, rights, order, rows, width):
    blocks = order.shape[0]
    in_specs = [pl.BlockSpec((rows, part.shape[1]), lambda step, order_ref: (order_ref[step], 0)) for part in lefts]
    in_specs += [pl.BlockSpec(part.shape, lambda step, order_ref: (0, 0)) for part in rights]
    out_specs = pl.BlockSpec((rows, width), lambda step, order_ref: (step, 0))
    out_shape = jax.ShapeDtypeStruct((blocks * rows, width), BF)
    operands = (*lefts, *rights)
    call = ordered_call(kernel, operands, in_specs, out_specs, out_shape, earlier, (blocks,), scalars=1, vmem=56)
    return call(order, *operands, *earlier)


def per_device(
    tokens,
    cotangent,
    seq_lengths,
    block_order,
    w_query,
    w_key,
    w_value,
    b_query,
    b_key,
    b_value,
    w_output,
    gain_attn,
    gain_mlp,
    w_gate,
    w_up,
    w_down,
):
    local_rows, width = tokens.shape
    sp_count = lax.axis_size("sp")
    sp_index = lax.axis_index("sp")
    fsdp_count = lax.axis_size("fsdp")
    group_rows = local_rows * sp_count
    block_rows = local_rows // 2
    query_width = H * HD
    key_width = KVH * HD
    hidden_all = w_gate.shape[1]
    hidden_width = hidden_all // fsdp_count
    shard_rows = w_gate.shape[0]
    widths = chunk_widths(hidden_width)

    vector_parts = [b_query, b_key, b_value, gain_attn, gain_mlp]
    vector_sizes = [part.shape[0] for part in vector_parts]
    vector_size = sum(vector_sizes)
    kv_columns = 2 * key_width
    vector_rows = round_up(-(-vector_size // kv_columns), 16)
    vector_pad = jnp.zeros((vector_rows * kv_columns - vector_size,), BF)
    kv_shard = jnp.concatenate(
        [
            jnp.concatenate([w_key, w_value], axis=1),
            jnp.concatenate(vector_parts + [vector_pad]).reshape(vector_rows, kv_columns),
        ],
        axis=0,
    )
    fsdp_index = lax.axis_index("fsdp")
    own_index = fsdp_index[None]
    kv_all, kv_hops = gather_small(kv_shard, own_index)
    kv_all = kv_all.reshape(fsdp_count, -1, kv_columns)
    w_kv = kv_all[:, :shard_rows].reshape(width, kv_columns)
    vectors = kv_all[:, shard_rows:].reshape(fsdp_count, -1).astype(F32)
    edges = [sum(vector_sizes[:n]) for n in range(len(vector_sizes) + 1)]
    bias_q, bias_k, bias_v, gain_one, gain_two = (
        vectors[:, edges[n] : edges[n + 1]].reshape(-1) for n in range(len(vector_sizes))
    )
    w_q, q_hops, q_far = gather_rows(w_query, own_index, *kv_hops)
    w_o, o_hops, o_far = gather_rows(w_output, own_index, *q_hops)

    cuts = cut_gate_up(w_gate, w_up, hidden_width, widths)

    def exchange(cut):
        return lax.all_to_all(cut, "fsdp", split_axis=0, concat_axis=0, tiled=True).reshape(width, -1)

    weights_first = exchange(after(cuts[0], *o_hops))

    order_row = block_order[0]
    local_pos = stream_positions(order_row, sp_index * local_rows, local_rows, block_rows)
    group_pos = stream_positions(order_row, 0, group_rows, block_rows)
    query_pos, key_pos = local_pos[:, None], group_pos[None, :]
    valid_rows = (local_pos < seq_lengths[0]).astype(F32)[:, None]
    upstream = cotangent.astype(F32)

    inputs = tokens.astype(F32)
    scale_one = lax.rsqrt(jnp.mean(inputs * inputs, axis=-1, keepdims=True) + EPS)
    unit_one = inputs * scale_one
    normed_one = (unit_one * gain_one).astype(BF)
    cosine, signed_sine = rotary_tables(local_pos)
    kv_lin = product(normed_one, w_kv)
    key_lin = kv_lin[:, :key_width] + bias_k
    key_rot = [
        (part * cosine + swap_halves(part) * signed_sine).astype(BF)
        for part in (key_lin[:, n * HD : (n + 1) * HD] for n in range(KVH))
    ]
    keys_values = jnp.concatenate(key_rot + [(kv_lin[:, key_width:] + bias_v).astype(BF)], axis=1)
    keys_values = lax.all_gather(keys_values, "sp", axis=0, tiled=True)
    query_lin = product(normed_one, w_q) + bias_q
    query_rot, mixed = attend_forward(query_lin, keys_values, cosine, signed_sine, query_pos, key_pos)
    attn_branch = product(mixed, w_o)
    hidden_in = inputs + valid_rows * attn_branch
    scale_two = lax.rsqrt(jnp.mean(hidden_in * hidden_in, axis=-1, keepdims=True) + EPS)
    unit_two = hidden_in * scale_two
    mlp_grad, grad_hops, grad_far = gather_rows((valid_rows * upstream).astype(BF), own_index, *o_far, weights_first)
    normed_two, two_hops, two_far = gather_rows((unit_two * gain_two).astype(BF), own_index)

    def rows_exchange(half):
        return lax.all_to_all(half, "fsdp", split_axis=0, concat_axis=0, tiled=True)

    def weight_term(left, right):
        return contract_first(left, right).astype(BF)

    def by_rows(term):
        return term.reshape(fsdp_count, shard_rows, -1)

    def block_order(other):
        if fsdp_count != 8:
            return jnp.arange(fsdp_count, dtype=jnp.int32)
        return jnp.array(far_masks(other), jnp.int32) ^ fsdp_index

    first_wide, last_wide = (round_up(wide, LANES) for wide in widths)
    down = jnp.pad(w_down, ((0, first_wide + last_wide - hidden_width), (0, 0)))
    weights_last = exchange(after(cuts[1], *grad_far, *two_far))
    both_weights = [weights_first, weights_last]
    order_other, order_same = block_order(True), block_order(False)
    line = Line(seq_lengths[0] > 0)

    def weight_step(left, right, rows=True):
        def work():
            term = weight_term(left, right)
            return by_rows(term) if rows else term

        return line.step(work)

    def add(left, right, *arrived):
        return line.kernel(lambda earlier: add_low(earlier, left, right), *arrived)

    def split(same, moved, *arrived):
        return line.kernel(lambda earlier: split_sum(earlier, same, moved), *arrived)

    def mix(begun, moved, *arrived):
        return line.kernel(lambda earlier: mix_sum(earlier, begun, moved), *arrived)

    def row_step(kernel, lefts, rights, order, *arrived):
        return line.kernel(
            lambda earlier: row_products(earlier, kernel, lefts, rights, order, local_rows, width), *arrived
        )

    hidden_1, grads_1 = line.kernel(lambda earlier: activate(earlier, normed_two, mlp_grad, weights_first, down, 0))
    def both_step(left, right, wide):
        def work():
            term = weight_term(left, right)
            return by_rows(term[:, :wide]), by_rows(term[:, wide:])

        return line.step(work)

    gate_term_1, up_term_1 = both_step(normed_two, grads_1, first_wide)
    gate_1_in, up_1_in = to_middle(gate_term_1), to_middle(up_term_1)
    hidden_2, grads_2 = line.kernel(
        lambda earlier: activate(earlier, normed_two, mlp_grad, weights_last, down, first_wide)
    )
    gate_2, up_2 = grads_2[:, :last_wide], grads_2[:, last_wide:]
    grads = [grads_1, grads_2]
    gate_1_sum = add(gate_term_1, gate_1_in)
    gate_1_across = across_middle(gate_1_sum)
    back_other = row_step(back_kernel, grads, both_weights, order_other)
    back_moved = from_core(back_other)
    back_same = row_step(back_kernel, grads, both_weights, order_same)
    back_begun = split(back_same, back_moved)
    back_far = from_far(back_begun)
    up_1_sum = add(up_term_1, up_1_in)
    up_1_across = across_middle(up_1_sum)
    gate_1_total = rows_exchange(add(gate_1_sum, gate_1_across))
    down_1 = weight_step(hidden_1, mlp_grad, False)
    down_1_in = to_middle(down_1)
    back_sent = mix(back_begun, back_far)
    back_parts = from_near(back_sent)
    down_2 = weight_step(hidden_2, mlp_grad, False)
    up_1_total = add(up_1_sum, up_1_across, gate_1_total)
    gate_1_ends = to_ends(gate_1_total)
    up_1_total = rows_exchange(up_1_total)
    down_2_in = to_middle(down_2)
    branch = row_step(branch_kernel, [hidden_1, hidden_2], [down], jnp.arange(fsdp_count, dtype=jnp.int32))
    branch = lax.psum_scatter(branch, "fsdp", scatter_dimension=0, tiled=True)

    def norm_step():
        gain_grad, back = norm_backward(sum_parts(back_parts), unit_two, gain_two, scale_two)
        hidden_in_grad = upstream + back
        attn_grad = (valid_rows * hidden_in_grad).astype(BF)
        return gain_grad, hidden_in_grad, attn_grad, contract_last(attn_grad, w_o).astype(BF)

    gain_two_grad, hidden_in_grad, attn_grad, mixed_grad = line.step(norm_step)

    def attend_step(number, *arrived):
        query_grad, pair = line.kernel(
            lambda earlier: attend_backward(
                earlier, number, query_rot, mixed_grad, keys_values, cosine, signed_sine, query_pos, key_pos
            ),
            *arrived,
        )
        return query_grad, pair.reshape(sp_count, local_rows, 2 * HD)

    def pair_exchange(pair):
        return lax.all_to_all(pair, "sp", split_axis=0, concat_axis=0, tiled=True)

    down_1_sum = add(down_1, down_1_in, up_1_total, gate_1_ends)
    down_1_across = across_middle(down_1_sum)
    up_1_ends = to_ends(up_1_total)
    query_grad_0, pair_0 = attend_step(0)

    def scatter_weight(term):
        return lax.psum_scatter(term, "fsdp", scatter_dimension=0, tiled=True)

    down_2_sum = add(down_2, down_2_in)
    down_2_across = across_middle(down_2_sum)
    gate_term_2 = weight_step(normed_two, gate_2)
    gate_2_in = to_middle(gate_term_2)
    down_1_total = add(down_1_sum, down_1_across, up_1_ends)
    down_1_ends = to_ends(down_1_total)
    query_grad_1, pair_1 = attend_step(1)
    pairs = pair_exchange(jnp.concatenate([pair_0, pair_1], axis=2))

    def kv_part(pair):
        pair_total = jnp.sum(pair.astype(F32), axis=0)
        part = pair_total[:, :HD]
        return (part * cosine - swap_halves(part) * signed_sine).astype(BF), pair_total[:, HD:].astype(BF)

    def query_step():
        query_lin_grad = jnp.concatenate([query_grad_0, query_grad_1], axis=1)
        sums = jnp.sum(query_lin_grad.astype(F32), axis=0)
        return weight_term(normed_one, query_lin_grad), contract_last(query_lin_grad, w_q), sums

    output_term = line.step(lambda: weight_term(mixed, attn_grad), branch)
    output_share = scatter_weight(output_term)
    query_term, normed_one_first, query_sums = line.step(query_step)
    query_share = scatter_weight(query_term)
    down_2_total = add(down_2_sum, down_2_across, down_1_ends)
    down_2_ends = to_ends(down_2_total)
    gate_2_sum = add(gate_term_2, gate_2_in)
    gate_2_across = across_middle(gate_2_sum)
    up_term_2 = weight_step(normed_two, up_2)
    up_2_in = to_middle(up_term_2)

    def kv_step():
        key_0, value_0 = kv_part(pairs[..., : 2 * HD])
        key_1, value_1 = kv_part(pairs[..., 2 * HD :])
        kv_lin_grad = jnp.concatenate([key_0, key_1, value_0, value_1], axis=1)
        normed_one_grad = normed_one_first + contract_last(kv_lin_grad, w_kv)
        gain_grad, back = norm_backward(normed_one_grad, unit_one, gain_one, scale_one)
        sums = jnp.sum(kv_lin_grad.astype(F32), axis=0)
        return weight_term(normed_one, kv_lin_grad), gain_grad, hidden_in_grad + back, sums

    kv_term, gain_one_grad, input_grad, kv_sums = line.step(kv_step)

    def last_rows(vector):
        return vector.reshape(fsdp_count, -1)

    extra_rows = 32

    marks = line.marks

    def pack_step():
        mlp_branch = branch.astype(F32)
        result = hidden_in + valid_rows * mlp_branch
        stat_parts = jnp.stack(
            [
                jnp.sum(valid_rows * result * result),
                jnp.sum(valid_rows * attn_branch * attn_branch),
                jnp.sum(valid_rows * mlp_branch * mlp_branch),
                jnp.sum(valid_rows),
            ]
        )
        vector_sums = jnp.concatenate(
            [
                last_rows(query_sums),
                last_rows(kv_sums[:key_width]),
                last_rows(kv_sums[key_width:]),
                last_rows(gain_one_grad),
                last_rows(gain_two_grad),
                jnp.broadcast_to(stat_parts[None, :], (fsdp_count, 4)),
                jnp.broadcast_to(jnp.concatenate(marks)[None, :].astype(F32), (fsdp_count, len(marks))),
            ],
            axis=1,
        ).astype(BF)
        extra = jnp.pad(vector_sums, ((0, 0), (0, extra_rows * kv_columns - vector_sums.shape[1])))
        packed = jnp.concatenate(
            [
                kv_term.reshape(fsdp_count, shard_rows, kv_columns),
                extra.reshape(fsdp_count, extra_rows, kv_columns),
            ],
            axis=1,
        )
        return packed.reshape(-1, kv_columns), result.astype(BF)

    packed, layer_out = line.step(pack_step)
    kv_share = scatter_weight(packed)
    gate_2_total = rows_exchange(add(gate_2_sum, gate_2_across, down_2_ends))
    up_2_sum = add(up_term_2, up_2_in)
    up_2_across = across_middle(up_2_sum)
    output_in = to_middle(output_share)

    def down_step():
        rows = [pick_sum(down_1_total, down_1_ends)[: widths[0]], pick_sum(down_2_total, down_2_ends)[: widths[1]]]
        return jnp.concatenate(rows, axis=0).astype(F32)

    grad_down = line.step(down_step, gate_2_total)
    gate_2_ends = to_ends(gate_2_total)
    output_sum = add(output_share, output_in)
    output_across = across_middle(output_sum)
    query_in = to_middle(query_share)
    up_2_total = rows_exchange(add(up_2_sum, up_2_across))
    kv_in = to_middle(kv_share)
    query_sum = add(query_share, query_in)
    query_across = across_middle(query_sum)
    output_total = add(output_sum, output_across)
    output_ends = to_ends(output_total)
    kv_sum = add(kv_share, kv_in, up_2_total)
    up_2_ends = to_ends(up_2_total)
    kv_across = across_middle(kv_sum)
    gate = (gate_1_total, gate_1_ends), (gate_2_total, gate_2_ends)
    up = (up_1_total, up_1_ends), (up_2_total, up_2_ends)
    query_total = add(query_sum, query_across)
    query_ends = to_ends(query_total)
    kv_total = add(kv_sum, kv_across)
    kv_ends = to_ends(kv_total)
    grad_gate = line.kernel(lambda earlier: join_columns(earlier, gate, (0, 0), hidden_width, widths))
    grad_up = line.kernel(lambda earlier: join_columns(earlier, up, (0, 0), hidden_width, widths))
    grad_output = pick_sum(output_total, output_ends).astype(F32)
    grad_query = pick_sum(query_total, query_ends).astype(F32)
    projections = pick_sum(kv_total, kv_ends).astype(F32)
    sums = projections[shard_rows:].reshape(-1)
    grad_b_query, grad_b_key, grad_b_value, grad_gain_one, grad_gain_two = (
        sums[edges[n] : edges[n + 1]] for n in range(len(vector_sizes))
    )
    stats = sums[edges[-1] : edges[-1] + 4]
    root_means = jnp.sqrt(stats[:3] / (stats[3] * width))

    return (
        layer_out,
        input_grad,
        grad_query,
        projections[:shard_rows, :key_width],
        projections[:shard_rows, key_width:],
        grad_b_query,
        grad_b_key,
        grad_b_value,
        grad_output,
        grad_gain_one,
        grad_gain_two,
        grad_gate,
        grad_up,
        grad_down,
        root_means,
    )


def solution(mesh):
    both, first = P(("fsdp", "sp"), None), P("fsdp", None)
    one = P("fsdp")
    in_specs = (both, both, one, first, first, first, first, one, one, one, first, one, one, first, first, first)
    out_specs = (both, both, first, first, first, one, one, one, first, one, one, first, first, first, P())
    return jax.shard_map(per_device, mesh=mesh, in_specs=in_specs, out_specs=out_specs, check_vma=False)
```

```python
import functools

import jax
import jax.numpy as jnp
from jax import lax
from jax.experimental import pallas as pl
from jax.experimental.pallas import tpu as pltpu
from jax.sharding import PartitionSpec as P

H = 12
KVH = 2
HD = 128
HEADS_STEP = 2
LANES = 128


EPS = 1e-06
THETA = 1000000.0
BF = jnp.bfloat16
F32 = jnp.float32


def rotary_tables(positions):
    half_width = HD // 2
    inverse = THETA ** (-(jnp.arange(half_width, dtype=F32) * 2.0) / HD)
    angles = positions.astype(F32)[:, None] * inverse[None, :]
    cosine, sine = jnp.cos(angles), jnp.sin(angles)
    return (
        jnp.concatenate([cosine, cosine], axis=-1),
        jnp.concatenate([-sine, sine], axis=-1),
    )


def swap_halves(values):
    half_width = HD // 2
    return jnp.concatenate([values[..., half_width:], values[..., :half_width]], axis=-1)


def stream_positions(order_row, first_row, row_count, block_size):
    row_ids = first_row + jnp.arange(row_count, dtype=jnp.int32)
    which_block = row_ids // block_size
    matches = jnp.arange(order_row.shape[0], dtype=jnp.int32)[None, :] == which_block[:, None]
    block_start = jnp.sum(jnp.where(matches, order_row[None, :], 0), axis=1)
    return block_start * block_size + row_ids % block_size


def norm_backward(normed_grad, unit_rows, gain_rows, scale_rows):
    gain_grad = jnp.sum(normed_grad * unit_rows, axis=0)
    scaled = normed_grad * gain_rows
    inner = jnp.mean(scaled * unit_rows, axis=-1, keepdims=True)
    return (gain_grad, scale_rows * (scaled - unit_rows * inner))


def contract_last(left, right):
    return lax.dot_general(left, right, (((1,), (1,)), ((), ())), preferred_element_type=F32)


def contract_first(left, right):
    return lax.dot_general(left, right, (((0,), (0,)), ((), ())), preferred_element_type=F32)


def product(left, right):
    return jnp.dot(left, right, preferred_element_type=F32)


def head_scores(query, keys, allowed):
    scores = contract_last(query, keys) * (HD ** (-0.5))
    scores = jnp.where(allowed, scores, -1e30)
    weights_exp = jnp.exp(scores - jnp.max(scores, axis=-1, keepdims=True))
    return weights_exp, 1.0 / jnp.sum(weights_exp, axis=-1, keepdims=True)


def attend_forward_kernel(
    query_lin, keys, values, cosine, signed_sine, query_pos, key_pos, query_rot, mixed
):
    allowed = key_pos[...] <= query_pos[...]
    for head in range(HEADS_STEP):
        columns = slice(head * HD, (head + 1) * HD)
        linear = query_lin[:, columns]
        rotated = linear * cosine[...] + pltpu.roll(linear, HD // 2, 1) * signed_sine[...]
        rotated = rotated.astype(BF)
        query_rot[:, columns] = rotated
        weights_exp, inverse_sum = head_scores(rotated, keys[...], allowed)
        probabilities = (weights_exp * inverse_sum).astype(BF)
        mixed[:, columns] = product(probabilities, values[...]).astype(BF)


def attend_forward(earlier, query_lin, keys_values, cosine, signed_sine, query_pos, key_pos):
    rows, width = query_lin.shape
    count_all = keys_values.shape[0]
    per_kv = H // KVH // HEADS_STEP
    wide = HEADS_STEP * HD
    table = pl.BlockSpec((rows, HD), lambda step: (0, 0))
    by_head = pl.BlockSpec((rows, wide), lambda step: (0, step))
    in_specs = [
        by_head,
        pl.BlockSpec((count_all, HD), lambda step: (0, step // per_kv)),
        pl.BlockSpec((count_all, HD), lambda step: (0, KVH + step // per_kv)),
        table,
        table,
        pl.BlockSpec((rows, 1), lambda step: (0, 0)),
        pl.BlockSpec((1, count_all), lambda step: (0, 0)),
    ]
    out_shape = [jax.ShapeDtypeStruct((rows, width), BF)] * 2
    operands = (query_lin, keys_values, keys_values, cosine, signed_sine, query_pos, key_pos)
    call = ordered_call(
        attend_forward_kernel, operands, in_specs, [by_head, by_head], out_shape, earlier, (H // HEADS_STEP,), vmem=48
    )
    return call(*operands, *earlier)


def attend_backward_kernel(
    query_rot, out_grad, keys, values, cosine, signed_sine, query_pos, key_pos, query_grad, pair_grad, key_sum, value_sum
):
    step = pl.program_id(0)
    allowed = key_pos[...] <= query_pos[...]
    scaling = HD ** (-0.5)

    @pl.when(step == 0)
    def _():
        key_sum[...] = jnp.zeros_like(key_sum)
        value_sum[...] = jnp.zeros_like(value_sum)

    for head in range(HEADS_STEP):
        columns = slice(head * HD, (head + 1) * HD)
        query = query_rot[:, columns]
        grad = out_grad[:, columns]
        weights_exp, inverse_sum = head_scores(query, keys[...], allowed)
        probabilities = weights_exp * inverse_sum
        prob_grad = contract_last(grad, values[...])
        weighted = jnp.sum(probabilities * prob_grad, axis=-1, keepdims=True)
        score_grad = (probabilities * (prob_grad - weighted)).astype(BF)
        turned = product(score_grad, keys[...]) * scaling
        turned = turned * cosine[...] - pltpu.roll(turned, HD // 2, 1) * signed_sine[...]
        query_grad[:, columns] = turned.astype(BF)
        key_sum[...] += contract_first(score_grad, query) * scaling
        value_sum[...] += contract_first(probabilities.astype(BF), grad)

    @pl.when(step == pl.num_programs(0) - 1)
    def _():
        pair_grad[:, :HD] = key_sum[...].astype(BF)
        pair_grad[:, HD:] = value_sum[...].astype(BF)


def attend_backward(earlier, number, query_rot, out_grad, keys_values, cosine, signed_sine, query_pos, key_pos):
    rows = query_rot.shape[0]
    count_all = keys_values.shape[0]
    per_kv = H // KVH // HEADS_STEP
    wide = HEADS_STEP * HD
    table = pl.BlockSpec((rows, HD), lambda step: (0, 0))
    by_head = pl.BlockSpec((rows, wide), lambda step: (0, number * per_kv + step))
    in_specs = [
        by_head,
        by_head,
        pl.BlockSpec((count_all, HD), lambda step: (0, number)),
        pl.BlockSpec((count_all, HD), lambda step: (0, KVH + number)),
        table,
        table,
        pl.BlockSpec((rows, 1), lambda step: (0, 0)),
        pl.BlockSpec((1, count_all), lambda step: (0, 0)),
    ]
    out_specs = [
        pl.BlockSpec((rows, wide), lambda step: (0, step)),
        pl.BlockSpec((count_all, 2 * HD), lambda step: (0, 0)),
    ]
    out_shape = [
        jax.ShapeDtypeStruct((rows, per_kv * wide), BF),
        jax.ShapeDtypeStruct((count_all, 2 * HD), BF),
    ]
    operands = (query_rot, out_grad, keys_values, keys_values, cosine, signed_sine, query_pos, key_pos)
    scratch = [pltpu.VMEM((count_all, HD), F32)] * 2
    call = ordered_call(
        attend_backward_kernel, operands, in_specs, out_specs, out_shape, earlier, (per_kv,), scratch=scratch, vmem=48
    )
    return call(*operands, *earlier)


def chunk_widths(hidden_width):
    first = max(LANES, hidden_width // (2 * LANES) * LANES)
    return [first, hidden_width - first]


def round_up(value, step):
    return (value + step - 1) // step * step


def cut_kernel(gate, up, out, *, hidden_width, offset, wide):
    padded = round_up(wide, LANES)
    for owner in range(gate.shape[1] // hidden_width):
        column = owner * hidden_width + offset
        first = column // LANES * LANES
        shift = column - first
        span = round_up(shift + wide, LANES)
        for half, source in enumerate((gate, up)):
            part = source[:, first : first + span].astype(F32)
            if shift:
                part = pltpu.roll(part, span - shift, 1)
            if span < padded:
                part = jnp.concatenate([part, jnp.zeros((part.shape[0], padded - span), F32)], axis=1)
            part = part[:, :padded]
            if wide < padded:
                lane = lax.broadcasted_iota(jnp.int32, part.shape, 1)
                part = jnp.where(lane < wide, part, 0.0)
            out[owner, :, half * padded : (half + 1) * padded] = part.astype(BF)


def cut_gate_up(earlier, w_gate, w_up, hidden_width, offset, wide):
    rows, total = w_gate.shape
    whole = pl.BlockSpec(memory_space=pltpu.VMEM)
    out_shape = jax.ShapeDtypeStruct((total // hidden_width, rows, 2 * round_up(wide, LANES)), BF)
    kernel = functools.partial(cut_kernel, hidden_width=hidden_width, offset=offset, wide=wide)
    call = ordered_call(kernel, (w_gate, w_up), [whole] * 2, whole, out_shape, earlier, vmem=48)
    return call(w_gate, w_up, *earlier)


def swap_fsdp(values, mask):
    count = lax.axis_size("fsdp")
    return lax.ppermute(values, "fsdp", [(i, i ^ mask) for i in range(count)])


COVER = 10**12


def ordered_call(kernel, operands, in_specs, out_specs, out_shape, earlier, grid=(), scalars=0, scratch=(), vmem=16):
    count = scalars + len(operands)

    def body(*refs):
        kernel(*refs[:count], *refs[count + len(earlier) :])

    return pl.pallas_call(
        body,
        grid_spec=pltpu.PrefetchScalarGridSpec(
            num_scalar_prefetch=scalars,
            grid=grid,
            in_specs=list(in_specs) + [pl.BlockSpec(memory_space=pl.ANY)] * len(earlier),
            out_specs=out_specs,
            scratch_shapes=scratch,
        ),
        out_shape=out_shape,
        compiler_params=pltpu.CompilerParams(vmem_limit_bytes=vmem * 1024 * 1024),
        cost_estimate=pl.CostEstimate(flops=COVER, bytes_accessed=1024, transcendentals=0),
    )


def spacer_kernel(out):
    out[...] = jnp.zeros_like(out)


def spacer(earlier):
    out_shape = jax.ShapeDtypeStruct((8, LANES), F32)
    return ordered_call(spacer_kernel, (), [], pl.BlockSpec(memory_space=pltpu.VMEM), out_shape, earlier)(*earlier)


def place_kernel(index, *refs, sizes):
    count = len(sizes)
    pieces, out, semaphores = refs[:count], refs[count], refs[count + 1]
    copies = []
    for number, (mask, first, size) in enumerate(sizes):
        start = jnp.bitwise_xor(index[0], mask) * (out.shape[0] // 8) + first
        target = out.at[pl.ds(pl.multiple_of(start, 16), size)]
        copies.append(pltpu.make_async_copy(pieces[number], target, semaphores.at[number]))
        copies[-1].start()
    for copy in copies:
        copy.wait()


def place_parts(earlier, parts, index):
    if not isinstance(parts, list):
        return parts
    rows = sum(part.shape[0] for _, _, part in parts)
    columns, dtype = parts[0][2].shape[1], parts[0][2].dtype
    sizes = [(mask, first, part.shape[0]) for mask, first, part in parts]
    in_specs = [pl.BlockSpec(memory_space=pltpu.SMEM)] + [pl.BlockSpec(memory_space=pl.ANY)] * len(parts)
    out_specs = pl.BlockSpec(memory_space=pltpu.VMEM)
    out_shape = jax.ShapeDtypeStruct((rows, columns), dtype)
    operands = (index, *(part for _, _, part in parts))
    scratch = [pltpu.SemaphoreType.DMA((len(parts),))]
    kernel = functools.partial(place_kernel, sizes=sizes)
    call = ordered_call(kernel, operands, in_specs, out_specs, out_shape, earlier, scratch=scratch, vmem=32)
    return call(*operands, *earlier)


def gather_rows(rows):
    if lax.axis_size("fsdp") != 8:
        return (rows,), lax.all_gather(rows, "fsdp", axis=0, tiled=True)
    half = rows.shape[0] // 2
    from_x = swap_fsdp(rows, 2)
    from_y = swap_fsdp(rows, 4)
    far_first = swap_fsdp(from_y[:half], 2)
    far_last = swap_fsdp(from_x[half:], 4)
    parts = []
    for mask, first, part in ((0, 0, rows), (2, 0, from_x), (4, 0, from_y), (6, 0, far_first), (6, half, far_last)):
        parts.append((mask, first, part))
        parts.append((mask ^ 1, first, swap_fsdp(part, 1)))
    return (from_x, from_y), parts


def gather_small(rows):
    if lax.axis_size("fsdp") != 8:
        return lax.all_gather(rows, "fsdp", axis=0, tiled=True)
    found = [(mask, rows if mask == 0 else swap_fsdp(rows, mask)) for mask in (0, 2, 4, 6)]
    parts = [(mask, 0, part) for mask, part in found]
    parts += [(mask ^ 1, 0, swap_fsdp(part, 1)) for mask, part in found]
    return parts


def hold_kernel(values, out):
    out[...] = values[...]


def hold(earlier, values):
    whole = pl.BlockSpec(memory_space=pltpu.VMEM)
    out_shape = jax.ShapeDtypeStruct(values.shape, values.dtype)
    return ordered_call(hold_kernel, (values,), [whole], whole, out_shape, earlier)(values, *earlier)


def mask_kernel(values, valid, out):
    out[...] = (values[...].astype(F32) * valid[...]).astype(BF)


def mask_rows(earlier, values, valid):
    whole = pl.BlockSpec(memory_space=pltpu.VMEM)
    out_shape = jax.ShapeDtypeStruct(values.shape, BF)
    return ordered_call(mask_kernel, (values, valid), [whole] * 2, whole, out_shape, earlier)(values, valid, *earlier)


class Line:
    def __init__(self, ready):
        self.ready = ready
        self.marks = []
        self.last = ()

    def fence(self):
        small = self.last[0]
        small = small[(0,) * (small.ndim - 2)][:16, :LANES]
        self.last = (swap_fsdp(small, 1),)

    def kernel(self, call, *arrived):
        found = call(self.last + arrived)
        self.last = (jax.tree.leaves(found)[0],)
        return found

    def step(self, work, *arrived):
        ready = self.ready
        arrived = self.last + arrived

        def marked():
            return work(), [array[(0,) * (array.ndim - 1)][:1] for array in arrived]

        shapes = jax.eval_shape(marked)

        def skip():
            return jnp.logical_not(ready), jax.tree.map(lambda leaf: jnp.zeros(leaf.shape, leaf.dtype), shapes)

        self.ready, (found, marks) = lax.cond(ready, lambda: (ready, marked()), skip)
        self.marks += marks
        self.last = (jax.tree.leaves(found)[0],)
        self.kernel(spacer)
        return found


def add_kernel(left, right, out):
    out[...] = (left[...].astype(F32) + right[...].astype(F32)).astype(BF)


def add_low(earlier, left, right):
    shape = left.shape
    columns = shape[-1]
    left, right = left.reshape(-1, columns), right.reshape(-1, columns)
    total = left.shape[0]
    rows = next(size for size in (768, 512, 384, 256, 192, 128, 64, 32, 16, total) if total % size == 0)
    block = pl.BlockSpec((rows, columns), lambda step: (step, 0))
    out_shape = jax.ShapeDtypeStruct(left.shape, BF)
    call = ordered_call(add_kernel, (left, right), [block] * 2, block, out_shape, earlier, (total // rows,), vmem=32)
    return call(left, right, *earlier).reshape(shape)


def split_kernel(same, other, own, to_x, to_y, far_first, far_last):
    rows = own.shape[0]
    half = rows // 2
    for first, out in ((0, own), (rows, to_x), (2 * rows, to_y), (3 * rows, far_first), (3 * rows + half, far_last)):
        size = out.shape[0]
        left, right = same[first : first + size], other[first : first + size]
        out[...] = (left.astype(F32) + right.astype(F32)).astype(BF)


def far_masks(other):
    return (1, 3, 5, 7) if other else (0, 2, 4, 6)


def pick_shards(partial, other):
    if partial.shape[0] != 8:
        return partial.reshape(-1, partial.shape[2])
    index = lax.axis_index("fsdp")
    parts = [lax.dynamic_index_in_dim(partial, index ^ mask, 0, keepdims=False) for mask in far_masks(other)]
    return jnp.concatenate(parts, axis=0)


def from_core(other):
    return swap_fsdp(other, 1) if lax.axis_size("fsdp") == 8 else other


def split_sum(earlier, same, moved):
    if lax.axis_size("fsdp") != 8:
        return [lax.psum_scatter(same, "fsdp", scatter_dimension=0, tiled=True)]
    rows, columns = same.shape[0] // 4, same.shape[1]
    sizes = (rows, rows, rows, rows // 2, rows // 2)
    whole = pl.BlockSpec(memory_space=pltpu.VMEM)
    out_shape = [jax.ShapeDtypeStruct((size, columns), BF) for size in sizes]
    call = ordered_call(split_kernel, (same, moved), [whole] * 2, [whole] * 5, out_shape, earlier, vmem=32)
    return call(same, moved, *earlier)


def from_far(begun):
    return [swap_fsdp(begun[3], 2), swap_fsdp(begun[4], 4)] if len(begun) == 5 else begun


def mix_kernel(to_x, to_y, by_x, by_y, out_x, out_y):
    half = by_x.shape[0]
    out_x[:half] = to_x[:half]
    out_x[half:] = (to_x[half:].astype(F32) + by_y[...].astype(F32)).astype(BF)
    out_y[:half] = (to_y[:half].astype(F32) + by_x[...].astype(F32)).astype(BF)
    out_y[half:] = to_y[half:]


def mix_sum(earlier, begun, moved):
    if len(begun) != 5:
        return begun
    own, to_x, to_y = begun[:3]
    whole = pl.BlockSpec(memory_space=pltpu.VMEM)
    out_shape = [jax.ShapeDtypeStruct(to_x.shape, BF)] * 2
    operands = (to_x, to_y, *moved)
    call = ordered_call(mix_kernel, operands, [whole] * 4, [whole] * 2, out_shape, earlier, vmem=32)
    return [own] + list(call(*operands, *earlier))


def from_near(sent):
    return [sent[0], swap_fsdp(sent[1], 2), swap_fsdp(sent[2], 4)] if len(sent) == 3 else sent


def sum_kernel(*refs):
    total = refs[0][...].astype(F32)
    for part in refs[1:-1]:
        total = total + part[...].astype(F32)
    refs[-1][...] = total.astype(BF)


def sum_low(earlier, parts):
    whole = pl.BlockSpec(memory_space=pltpu.VMEM)
    out_shape = jax.ShapeDtypeStruct(parts[0].shape, BF)
    call = ordered_call(sum_kernel, tuple(parts), [whole] * len(parts), whole, out_shape, earlier, vmem=32)
    return call(*parts, *earlier)


def sum_parts(parts):
    total = parts[0].astype(F32)
    for part in parts[1:]:
        total = total + part.astype(F32)
    return total


def to_middle(values):
    return lax.ppermute(values, "sp", [(0, 1), (3, 2)])


def across_middle(values):
    return lax.ppermute(values, "sp", [(1, 2), (2, 1)])


def to_ends(values):
    return lax.ppermute(values, "sp", [(1, 0), (2, 3)])


def pick_sum(total, moved):
    place = lax.axis_index("sp")
    return jnp.where((place == 1) | (place == 2), total, moved)


def join_kernel(middle, *refs, hidden_width, widths):
    out = refs[-1]
    chunks = [refs[2 * n : 2 * n + 2] for n in range(len(widths))]
    total = out.shape[1]

    def fill(number):
        for owner in range(total // hidden_width):
            column = owner * hidden_width
            for chunk, wide in zip(chunks, widths):
                part = chunk[number][owner].astype(F32)
                first = column // LANES * LANES
                shift = column - first
                span = round_up(shift + wide, LANES)
                if span > part.shape[1]:
                    part = jnp.concatenate([part, jnp.zeros((part.shape[0], span - part.shape[1]), F32)], axis=1)
                if shift:
                    part = pltpu.roll(part, shift, 1)
                    lane = lax.broadcasted_iota(jnp.int32, (part.shape[0], LANES), 1)
                    head = jnp.where(lane >= shift, part[:, :LANES], out[:, first : first + LANES])
                    out[:, first : first + LANES] = head
                    if span > LANES:
                        out[:, first + LANES : first + span] = part[:, LANES:span]
                else:
                    out[:, first : first + span] = part[:, :span]
                column += wide

    @pl.when(middle[0] == 1)
    def _():
        fill(0)

    @pl.when(middle[0] == 0)
    def _():
        fill(1)


def join_columns(earlier, found, columns, hidden_width, widths):
    place = lax.axis_index("sp")
    middle = ((place == 1) | (place == 2)).astype(jnp.int32)[None]
    arrays = [part for chunk in found for part in chunk]
    count, total = arrays[0].shape[:2]
    rows = 16
    in_specs = [pl.BlockSpec(memory_space=pltpu.SMEM)]
    for wide, column in zip(widths, columns):
        block = pl.BlockSpec((count, rows, round_up(wide, LANES)), lambda block, column=column: (0, block, column))
        in_specs += [block, block]
    out_specs = pl.BlockSpec((rows, count * hidden_width), lambda block: (block, 0))
    out_shape = jax.ShapeDtypeStruct((total, count * hidden_width), F32)
    operands = (middle, *arrays)
    kernel = functools.partial(join_kernel, hidden_width=hidden_width, widths=widths)
    call = ordered_call(kernel, operands, in_specs, out_specs, out_shape, earlier, (total // rows,), vmem=32)
    return call(*operands, *earlier)


def stack_kernel(middle, *refs):
    out, chunks = refs[-1], refs[:-1]

    def fill(number):
        first = 0
        for n in range(len(chunks) // 2):
            rows = min(chunks[2 * n].shape[0], out.shape[0] - first)
            out[first : first + rows] = chunks[2 * n + number][:rows].astype(F32)
            first += rows

    @pl.when(middle[0] == 1)
    def _():
        fill(0)

    @pl.when(middle[0] == 0)
    def _():
        fill(1)


def stack_rows(earlier, found, rows):
    place = lax.axis_index("sp")
    middle = ((place == 1) | (place == 2)).astype(jnp.int32)[None]
    arrays = [part for chunk in found for part in chunk]
    whole = pl.BlockSpec(memory_space=pltpu.VMEM)
    in_specs = [pl.BlockSpec(memory_space=pltpu.SMEM)] + [whole] * len(arrays)
    out_shape = jax.ShapeDtypeStruct((rows, arrays[0].shape[1]), F32)
    operands = (middle, *arrays)
    return ordered_call(stack_kernel, operands, in_specs, whole, out_shape, earlier, vmem=40)(*operands, *earlier)


def activate_kernel(normed, grad, weights, down, hidden_out, grads_out, *, first):
    padded = weights.shape[1] // 2
    rows = normed[...]
    gate = product(rows, weights[:, :padded])
    up = product(rows, weights[:, padded:])
    hidden_grad = contract_last(grad[...], down[first : first + padded])
    sigma = 1.0 / (1.0 + jnp.exp(-gate))
    activated = gate * sigma
    hidden_out[...] = (activated * up).astype(BF)
    grads_out[:, :padded] = (hidden_grad * up * (sigma * (1.0 + gate * (1.0 - sigma)))).astype(BF)
    grads_out[:, padded:] = (hidden_grad * activated).astype(BF)


def activate(earlier, normed, grad, weights, down, first):
    total, width = normed.shape
    wide = weights.shape[1] // 2
    rows = 256
    by_rows = pl.BlockSpec((rows, width), lambda step: (step, 0))
    in_specs = [
        by_rows,
        by_rows,
        pl.BlockSpec(weights.shape, lambda step: (0, 0)),
        pl.BlockSpec(down.shape, lambda step: (0, 0)),
    ]
    out_specs = [pl.BlockSpec((rows, wide * n), lambda step: (step, 0)) for n in (1, 2)]
    out_shape = [jax.ShapeDtypeStruct((total, wide * n), BF) for n in (1, 2)]
    operands = (normed, grad, weights, down)
    kernel = functools.partial(activate_kernel, first=first)
    call = ordered_call(kernel, operands, in_specs, out_specs, out_shape, earlier, (total // rows,), vmem=56)
    return call(*operands, *earlier)


def back_kernel(order, grads_1, grads_2, weights_1, weights_2, out):
    total = contract_last(grads_1[...], weights_1[...]) + contract_last(grads_2[...], weights_2[...])
    out[...] = total.astype(BF)


def branch_kernel(order, hidden_1, hidden_2, down, out):
    first = hidden_1.shape[1]
    total = product(hidden_1[...], down[:first]) + product(hidden_2[...], down[first:])
    out[...] = total.astype(BF)


def row_products(earlier, kernel, lefts, rights, order, rows, width):
    blocks = order.shape[0]
    in_specs = [pl.BlockSpec((rows, part.shape[1]), lambda step, order_ref: (order_ref[step], 0)) for part in lefts]
    in_specs += [pl.BlockSpec(part.shape, lambda step, order_ref: (0, 0)) for part in rights]
    out_specs = pl.BlockSpec((rows, width), lambda step, order_ref: (step, 0))
    out_shape = jax.ShapeDtypeStruct((blocks * rows, width), BF)
    operands = (*lefts, *rights)
    call = ordered_call(kernel, operands, in_specs, out_specs, out_shape, earlier, (blocks,), scalars=1, vmem=56)
    return call(order, *operands, *earlier)


def per_device(
    tokens,
    cotangent,
    seq_lengths,
    block_order,
    w_query,
    w_key,
    w_value,
    b_query,
    b_key,
    b_value,
    w_output,
    gain_attn,
    gain_mlp,
    w_gate,
    w_up,
    w_down,
):
    local_rows, width = tokens.shape
    sp_count = lax.axis_size("sp")
    sp_index = lax.axis_index("sp")
    fsdp_count = lax.axis_size("fsdp")
    group_rows = local_rows * sp_count
    block_rows = local_rows // 2
    query_width = H * HD
    key_width = KVH * HD
    hidden_all = w_gate.shape[1]
    hidden_width = hidden_all // fsdp_count
    shard_rows = w_gate.shape[0]
    widths = chunk_widths(hidden_width)

    vector_parts = [b_query, b_key, b_value, gain_attn, gain_mlp]
    vector_sizes = [part.shape[0] for part in vector_parts]
    vector_size = sum(vector_sizes)
    kv_columns = 2 * key_width
    vector_rows = round_up(-(-vector_size // kv_columns), 16)
    vector_pad = jnp.zeros((vector_rows * kv_columns - vector_size,), BF)
    kv_shard = jnp.concatenate(
        [
            jnp.concatenate([w_key, w_value], axis=1),
            jnp.concatenate(vector_parts + [vector_pad]).reshape(vector_rows, kv_columns),
        ],
        axis=0,
    )
    fsdp_index = lax.axis_index("fsdp")
    own_index = fsdp_index[None]
    line = Line(seq_lengths[0] > 0)

    def exchange(cut):
        return lax.all_to_all(cut, "fsdp", split_axis=0, concat_axis=0, tiled=True).reshape(width, -1)

    def cut(first, wide, *arrived):
        return line.kernel(lambda earlier: cut_gate_up(earlier, w_gate, w_up, hidden_width, first, wide), *arrived)

    def place(parts, *arrived):
        return line.kernel(lambda earlier: place_parts(earlier, parts, own_index), *arrived)

    kv_parts = gather_small(kv_shard)
    q_hops, q_parts = gather_rows(line.kernel(lambda earlier: hold(earlier, w_query), kv_shard))
    kv_all = place(kv_parts)
    kv_all = kv_all.reshape(fsdp_count, -1, kv_columns)
    w_kv = kv_all[:, :shard_rows].reshape(width, kv_columns)
    vectors = kv_all[:, shard_rows:].reshape(fsdp_count, -1).astype(F32)
    edges = [sum(vector_sizes[:n]) for n in range(len(vector_sizes) + 1)]
    bias_q, bias_k, bias_v, gain_one, gain_two = (
        vectors[:, edges[n] : edges[n + 1]].reshape(-1) for n in range(len(vector_sizes))
    )
    order_row = block_order[0]
    local_pos = stream_positions(order_row, sp_index * local_rows, local_rows, block_rows)
    group_pos = stream_positions(order_row, 0, group_rows, block_rows)
    query_pos, key_pos = local_pos[:, None], group_pos[None, :]
    valid_rows = (local_pos < seq_lengths[0]).astype(F32)[:, None]
    upstream = cotangent.astype(F32)

    inputs = tokens.astype(F32)
    scale_one = lax.rsqrt(jnp.mean(inputs * inputs, axis=-1, keepdims=True) + EPS)
    unit_one = inputs * scale_one
    normed_one = (unit_one * gain_one).astype(BF)
    cosine, signed_sine = rotary_tables(local_pos)
    kv_lin = product(normed_one, w_kv)
    key_lin = kv_lin[:, :key_width] + bias_k
    key_rot = [
        (part * cosine + swap_halves(part) * signed_sine).astype(BF)
        for part in (key_lin[:, n * HD : (n + 1) * HD] for n in range(KVH))
    ]
    keys_values = jnp.concatenate(key_rot + [(kv_lin[:, key_width:] + bias_v).astype(BF)], axis=1)
    keys_values = lax.all_gather(keys_values, "sp", axis=0, tiled=True)
    o_hops, o_parts = gather_rows(line.kernel(lambda earlier: hold(earlier, w_output), *q_hops))
    w_q = place(q_parts)
    query_lin = product(normed_one, w_q) + bias_q
    grad_rows = line.kernel(lambda earlier: mask_rows(earlier, cotangent, valid_rows), *o_hops)
    grad_hops, grad_parts = gather_rows(grad_rows)
    weights_first = exchange(cut(0, widths[0]))
    query_rot, mixed = line.kernel(
        lambda earlier: attend_forward(earlier, query_lin, keys_values, cosine, signed_sine, query_pos, key_pos)
    )
    w_o = place(o_parts)
    attn_branch = product(mixed, w_o)
    hidden_in = inputs + valid_rows * attn_branch
    scale_two = lax.rsqrt(jnp.mean(hidden_in * hidden_in, axis=-1, keepdims=True) + EPS)
    unit_two = hidden_in * scale_two
    two_hops, two_parts = gather_rows((unit_two * gain_two).astype(BF))
    mlp_grad = place(grad_parts, weights_first, *two_hops)
    weights_last = exchange(cut(widths[0], widths[1]))
    normed_two = place(two_parts)

    def rows_exchange(half):
        return lax.all_to_all(half, "fsdp", split_axis=0, concat_axis=0, tiled=True)

    def weight_term(left, right):
        return contract_first(left, right).astype(BF)

    def by_rows(term):
        return term.reshape(fsdp_count, shard_rows, -1)

    def block_order(other):
        if fsdp_count != 8:
            return jnp.arange(fsdp_count, dtype=jnp.int32)
        return jnp.array(far_masks(other), jnp.int32) ^ fsdp_index

    first_wide, last_wide = (round_up(wide, LANES) for wide in widths)
    down = jnp.pad(w_down, ((0, first_wide + last_wide - hidden_width), (0, 0)))
    both_weights = [weights_first, weights_last]
    order_other, order_same = block_order(True), block_order(False)

    def weight_step(left, right, rows=True):
        def work():
            term = weight_term(left, right)
            return by_rows(term) if rows else term

        return line.step(work)

    def add(left, right, *arrived):
        return line.kernel(lambda earlier: add_low(earlier, left, right), *arrived)

    def split(same, moved, *arrived):
        return line.kernel(lambda earlier: split_sum(earlier, same, moved), *arrived)

    def mix(begun, moved, *arrived):
        return line.kernel(lambda earlier: mix_sum(earlier, begun, moved), *arrived)

    def row_step(kernel, lefts, rights, order, *arrived):
        return line.kernel(
            lambda earlier: row_products(earlier, kernel, lefts, rights, order, local_rows, width), *arrived
        )

    hidden_1, grads_1 = line.kernel(lambda earlier: activate(earlier, normed_two, mlp_grad, weights_first, down, 0))
    def both_step(left, right, wide):
        def work():
            term = weight_term(left, right)
            return by_rows(term[:, :wide]), by_rows(term[:, wide:])

        return line.step(work)

    gate_term_1, up_term_1 = both_step(normed_two, grads_1, first_wide)
    gate_1_in, up_1_in = to_middle(gate_term_1), to_middle(up_term_1)
    hidden_2, grads_2 = line.kernel(
        lambda earlier: activate(earlier, normed_two, mlp_grad, weights_last, down, first_wide)
    )
    gate_2, up_2 = grads_2[:, :last_wide], grads_2[:, last_wide:]
    grads = [grads_1, grads_2]
    gate_1_sum = add(gate_term_1, gate_1_in)
    gate_1_across = across_middle(gate_1_sum)
    back_other = row_step(back_kernel, grads, both_weights, order_other)
    back_moved = from_core(back_other)
    back_same = row_step(back_kernel, grads, both_weights, order_same)
    back_begun = split(back_same, back_moved)
    back_far = from_far(back_begun)
    up_1_sum = add(up_term_1, up_1_in)
    up_1_across = across_middle(up_1_sum)
    gate_1_total = rows_exchange(add(gate_1_sum, gate_1_across))
    down_1 = weight_step(hidden_1, mlp_grad, False)
    down_1_in = to_middle(down_1)
    back_sent = mix(back_begun, back_far)
    back_parts = from_near(back_sent)
    down_2 = weight_step(hidden_2, mlp_grad, False)
    up_1_total = add(up_1_sum, up_1_across, gate_1_total)
    gate_1_ends = to_ends(gate_1_total)
    up_1_total = rows_exchange(up_1_total)
    down_2_in = to_middle(down_2)
    branch = row_step(branch_kernel, [hidden_1, hidden_2], [down], jnp.arange(fsdp_count, dtype=jnp.int32))
    branch = lax.psum_scatter(branch, "fsdp", scatter_dimension=0, tiled=True)

    def norm_step():
        gain_grad, back = norm_backward(sum_parts(back_parts), unit_two, gain_two, scale_two)
        hidden_in_grad = upstream + back
        attn_grad = (valid_rows * hidden_in_grad).astype(BF)
        return gain_grad, hidden_in_grad, attn_grad, contract_last(attn_grad, w_o).astype(BF)

    gain_two_grad, hidden_in_grad, attn_grad, mixed_grad = line.step(norm_step)

    def attend_step(number, *arrived):
        query_grad, pair = line.kernel(
            lambda earlier: attend_backward(
                earlier, number, query_rot, mixed_grad, keys_values, cosine, signed_sine, query_pos, key_pos
            ),
            *arrived,
        )
        return query_grad, pair.reshape(sp_count, local_rows, 2 * HD)

    def pair_exchange(pair):
        return lax.all_to_all(pair, "sp", split_axis=0, concat_axis=0, tiled=True)

    down_1_sum = add(down_1, down_1_in, up_1_total, gate_1_ends)
    down_1_across = across_middle(down_1_sum)
    up_1_ends = to_ends(up_1_total)
    query_grad_0, pair_0 = attend_step(0)

    def scatter_weight(term):
        return lax.psum_scatter(term, "fsdp", scatter_dimension=0, tiled=True)

    down_2_sum = add(down_2, down_2_in)
    down_2_across = across_middle(down_2_sum)
    gate_term_2 = weight_step(normed_two, gate_2)
    gate_2_in = to_middle(gate_term_2)
    down_1_total = add(down_1_sum, down_1_across)
    down_1_ends = to_ends(down_1_total)
    output_term = line.step(lambda: weight_term(mixed, attn_grad), branch)
    output_share = scatter_weight(output_term)
    query_grad_1, pair_1 = attend_step(1)
    pairs = pair_exchange(jnp.concatenate([pair_0, pair_1], axis=2))
    gate_2_sum = add(gate_term_2, gate_2_in)
    gate_2_across = across_middle(gate_2_sum)
    line.fence()

    def kv_part(pair):
        pair_total = jnp.sum(pair.astype(F32), axis=0)
        part = pair_total[:, :HD]
        return (part * cosine - swap_halves(part) * signed_sine).astype(BF), pair_total[:, HD:].astype(BF)

    def query_step():
        query_lin_grad = jnp.concatenate([query_grad_0, query_grad_1], axis=1)
        sums = jnp.sum(query_lin_grad.astype(F32), axis=0)
        return weight_term(normed_one, query_lin_grad), contract_last(query_lin_grad, w_q), sums

    query_term, normed_one_first, query_sums = line.step(query_step)
    query_share = scatter_weight(query_term)
    up_term_2 = weight_step(normed_two, up_2)
    up_2_in = to_middle(up_term_2)
    down_2_total = add(down_2_sum, down_2_across)
    down_2_ends = to_ends(down_2_total)
    gate_2_total = rows_exchange(add(gate_2_sum, gate_2_across, up_1_ends))

    def kv_step():
        key_0, value_0 = kv_part(pairs[..., : 2 * HD])
        key_1, value_1 = kv_part(pairs[..., 2 * HD :])
        kv_lin_grad = jnp.concatenate([key_0, key_1, value_0, value_1], axis=1)
        normed_one_grad = normed_one_first + contract_last(kv_lin_grad, w_kv)
        gain_grad, back = norm_backward(normed_one_grad, unit_one, gain_one, scale_one)
        sums = jnp.sum(kv_lin_grad.astype(F32), axis=0)
        return weight_term(normed_one, kv_lin_grad), gain_grad, hidden_in_grad + back, sums

    kv_term, gain_one_grad, input_grad, kv_sums = line.step(kv_step)

    def last_rows(vector):
        return vector.reshape(fsdp_count, -1)

    extra_rows = 32

    marks = line.marks

    def pack_step():
        mlp_branch = branch.astype(F32)
        result = hidden_in + valid_rows * mlp_branch
        stat_parts = jnp.stack(
            [
                jnp.sum(valid_rows * result * result),
                jnp.sum(valid_rows * attn_branch * attn_branch),
                jnp.sum(valid_rows * mlp_branch * mlp_branch),
                jnp.sum(valid_rows),
            ]
        )
        vector_sums = jnp.concatenate(
            [
                last_rows(query_sums),
                last_rows(kv_sums[:key_width]),
                last_rows(kv_sums[key_width:]),
                last_rows(gain_one_grad),
                last_rows(gain_two_grad),
                jnp.broadcast_to(stat_parts[None, :], (fsdp_count, 4)),
                jnp.broadcast_to(jnp.concatenate(marks)[None, :].astype(F32), (fsdp_count, len(marks))),
            ],
            axis=1,
        ).astype(BF)
        extra = jnp.pad(vector_sums, ((0, 0), (0, extra_rows * kv_columns - vector_sums.shape[1])))
        packed = jnp.concatenate(
            [
                kv_term.reshape(fsdp_count, shard_rows, kv_columns),
                extra.reshape(fsdp_count, extra_rows, kv_columns),
            ],
            axis=1,
        )
        return packed.reshape(-1, kv_columns), result.astype(BF)

    packed, layer_out = line.step(pack_step)
    kv_share = scatter_weight(packed)
    up_2_sum = add(up_term_2, up_2_in, gate_2_total)
    gate_2_ends = to_ends(gate_2_total)
    up_2_across = across_middle(up_2_sum)
    output_in = to_middle(output_share)

    down = (down_1_total, down_1_ends), (down_2_total, down_2_ends)
    grad_down = line.kernel(lambda earlier: stack_rows(earlier, down, hidden_width))
    output_sum = add(output_share, output_in)
    output_across = across_middle(output_sum)
    query_in = to_middle(query_share)
    up_2_total = rows_exchange(add(up_2_sum, up_2_across))
    kv_in = to_middle(kv_share)
    query_sum = add(query_share, query_in)
    query_across = across_middle(query_sum)
    output_total = add(output_sum, output_across)
    output_ends = to_ends(output_total)
    kv_sum = add(kv_share, kv_in, up_2_total)
    up_2_ends = to_ends(up_2_total)
    kv_across = across_middle(kv_sum)
    gate = (gate_1_total, gate_1_ends), (gate_2_total, gate_2_ends)
    up = (up_1_total, up_1_ends), (up_2_total, up_2_ends)
    query_total = add(query_sum, query_across)
    query_ends = to_ends(query_total)
    kv_total = add(kv_sum, kv_across)
    kv_ends = to_ends(kv_total)
    grad_gate = line.kernel(lambda earlier: join_columns(earlier, gate, (0, 0), hidden_width, widths))
    grad_up = line.kernel(lambda earlier: join_columns(earlier, up, (0, 0), hidden_width, widths))
    grad_output = pick_sum(output_total, output_ends).astype(F32)
    grad_query = pick_sum(query_total, query_ends).astype(F32)
    projections = pick_sum(kv_total, kv_ends).astype(F32)
    sums = projections[shard_rows:].reshape(-1)
    grad_b_query, grad_b_key, grad_b_value, grad_gain_one, grad_gain_two = (
        sums[edges[n] : edges[n + 1]] for n in range(len(vector_sizes))
    )
    stats = sums[edges[-1] : edges[-1] + 4]
    root_means = jnp.sqrt(stats[:3] / (stats[3] * width))

    return (
        layer_out,
        input_grad,
        grad_query,
        projections[:shard_rows, :key_width],
        projections[:shard_rows, key_width:],
        grad_b_query,
        grad_b_key,
        grad_b_value,
        grad_output,
        grad_gain_one,
        grad_gain_two,
        grad_gate,
        grad_up,
        grad_down,
        root_means,
    )


def solution(mesh):
    both, first = P(("fsdp", "sp"), None), P("fsdp", None)
    one = P("fsdp")
    in_specs = (both, both, one, first, first, first, first, one, one, one, first, one, one, first, first, first)
    out_specs = (both, both, first, first, first, one, one, one, first, one, one, first, first, first, P())
    return jax.shard_map(per_device, mesh=mesh, in_specs=in_specs, out_specs=out_specs, check_vma=False)
```

```python
import functools

import jax
import jax.numpy as jnp
from jax import lax
from jax.experimental import pallas as pl
from jax.experimental.pallas import tpu as pltpu
from jax.sharding import PartitionSpec as P

H = 12
KVH = 2
HD = 128
HEADS_STEP = 2
LANES = 128


EPS = 1e-06
THETA = 1000000.0
BF = jnp.bfloat16
F32 = jnp.float32


def rotary_tables(positions):
    half_width = HD // 2
    inverse = THETA ** (-(jnp.arange(half_width, dtype=F32) * 2.0) / HD)
    angles = positions.astype(F32)[:, None] * inverse[None, :]
    cosine, sine = jnp.cos(angles), jnp.sin(angles)
    return (
        jnp.concatenate([cosine, cosine], axis=-1),
        jnp.concatenate([-sine, sine], axis=-1),
    )


def swap_halves(values):
    half_width = HD // 2
    return jnp.concatenate([values[..., half_width:], values[..., :half_width]], axis=-1)


def stream_positions(order_row, first_row, row_count, block_size):
    row_ids = first_row + jnp.arange(row_count, dtype=jnp.int32)
    which_block = row_ids // block_size
    matches = jnp.arange(order_row.shape[0], dtype=jnp.int32)[None, :] == which_block[:, None]
    block_start = jnp.sum(jnp.where(matches, order_row[None, :], 0), axis=1)
    return block_start * block_size + row_ids % block_size


def norm_backward(normed_grad, unit_rows, gain_rows, scale_rows):
    gain_grad = jnp.sum(normed_grad * unit_rows, axis=0)
    scaled = normed_grad * gain_rows
    inner = jnp.mean(scaled * unit_rows, axis=-1, keepdims=True)
    return (gain_grad, scale_rows * (scaled - unit_rows * inner))


def contract_last(left, right):
    return lax.dot_general(left, right, (((1,), (1,)), ((), ())), preferred_element_type=F32)


def contract_first(left, right):
    return lax.dot_general(left, right, (((0,), (0,)), ((), ())), preferred_element_type=F32)


def product(left, right):
    return jnp.dot(left, right, preferred_element_type=F32)


def head_scores(query, keys, allowed):
    scores = contract_last(query, keys) * (HD ** (-0.5))
    scores = jnp.where(allowed, scores, -1e30)
    weights_exp = jnp.exp(scores - jnp.max(scores, axis=-1, keepdims=True))
    return weights_exp, 1.0 / jnp.sum(weights_exp, axis=-1, keepdims=True)


def attend_forward_kernel(
    query_lin, keys, values, cosine, signed_sine, query_pos, key_pos, query_rot, mixed
):
    allowed = key_pos[...] <= query_pos[...]
    for head in range(HEADS_STEP):
        columns = slice(head * HD, (head + 1) * HD)
        linear = query_lin[:, columns]
        rotated = linear * cosine[...] + pltpu.roll(linear, HD // 2, 1) * signed_sine[...]
        rotated = rotated.astype(BF)
        query_rot[:, columns] = rotated
        weights_exp, inverse_sum = head_scores(rotated, keys[...], allowed)
        probabilities = (weights_exp * inverse_sum).astype(BF)
        mixed[:, columns] = product(probabilities, values[...]).astype(BF)


def attend_forward(earlier, query_lin, keys_values, cosine, signed_sine, query_pos, key_pos):
    rows, width = query_lin.shape
    count_all = keys_values.shape[0]
    per_kv = H // KVH // HEADS_STEP
    wide = HEADS_STEP * HD
    table = pl.BlockSpec((rows, HD), lambda step: (0, 0))
    by_head = pl.BlockSpec((rows, wide), lambda step: (0, step))
    in_specs = [
        by_head,
        pl.BlockSpec((count_all, HD), lambda step: (0, step // per_kv)),
        pl.BlockSpec((count_all, HD), lambda step: (0, KVH + step // per_kv)),
        table,
        table,
        pl.BlockSpec((rows, 1), lambda step: (0, 0)),
        pl.BlockSpec((1, count_all), lambda step: (0, 0)),
    ]
    out_shape = [jax.ShapeDtypeStruct((rows, width), BF)] * 2
    operands = (query_lin, keys_values, keys_values, cosine, signed_sine, query_pos, key_pos)
    call = ordered_call(
        attend_forward_kernel, operands, in_specs, [by_head, by_head], out_shape, earlier, (H // HEADS_STEP,), vmem=48
    )
    return call(*operands, *earlier)


def attend_backward_kernel(
    query_rot, out_grad, keys, values, cosine, signed_sine, query_pos, key_pos, query_grad, pair_grad, key_sum, value_sum
):
    step = pl.program_id(0)
    allowed = key_pos[...] <= query_pos[...]
    scaling = HD ** (-0.5)

    @pl.when(step == 0)
    def _():
        key_sum[...] = jnp.zeros_like(key_sum)
        value_sum[...] = jnp.zeros_like(value_sum)

    for head in range(HEADS_STEP):
        columns = slice(head * HD, (head + 1) * HD)
        query = query_rot[:, columns]
        grad = out_grad[:, columns]
        weights_exp, inverse_sum = head_scores(query, keys[...], allowed)
        probabilities = weights_exp * inverse_sum
        prob_grad = contract_last(grad, values[...])
        weighted = jnp.sum(probabilities * prob_grad, axis=-1, keepdims=True)
        score_grad = (probabilities * (prob_grad - weighted)).astype(BF)
        turned = product(score_grad, keys[...]) * scaling
        turned = turned * cosine[...] - pltpu.roll(turned, HD // 2, 1) * signed_sine[...]
        query_grad[:, columns] = turned.astype(BF)
        key_sum[...] += contract_first(score_grad, query) * scaling
        value_sum[...] += contract_first(probabilities.astype(BF), grad)

    @pl.when(step == pl.num_programs(0) - 1)
    def _():
        pair_grad[:, :HD] = key_sum[...].astype(BF)
        pair_grad[:, HD:] = value_sum[...].astype(BF)


def attend_backward(earlier, number, query_rot, out_grad, keys_values, cosine, signed_sine, query_pos, key_pos):
    rows = query_rot.shape[0]
    count_all = keys_values.shape[0]
    per_kv = H // KVH // HEADS_STEP
    wide = HEADS_STEP * HD
    table = pl.BlockSpec((rows, HD), lambda step: (0, 0))
    by_head = pl.BlockSpec((rows, wide), lambda step: (0, number * per_kv + step))
    in_specs = [
        by_head,
        by_head,
        pl.BlockSpec((count_all, HD), lambda step: (0, number)),
        pl.BlockSpec((count_all, HD), lambda step: (0, KVH + number)),
        table,
        table,
        pl.BlockSpec((rows, 1), lambda step: (0, 0)),
        pl.BlockSpec((1, count_all), lambda step: (0, 0)),
    ]
    out_specs = [
        pl.BlockSpec((rows, wide), lambda step: (0, step)),
        pl.BlockSpec((count_all, 2 * HD), lambda step: (0, 0)),
    ]
    out_shape = [
        jax.ShapeDtypeStruct((rows, per_kv * wide), BF),
        jax.ShapeDtypeStruct((count_all, 2 * HD), BF),
    ]
    operands = (query_rot, out_grad, keys_values, keys_values, cosine, signed_sine, query_pos, key_pos)
    scratch = [pltpu.VMEM((count_all, HD), F32)] * 2
    call = ordered_call(
        attend_backward_kernel, operands, in_specs, out_specs, out_shape, earlier, (per_kv,), scratch=scratch, vmem=48
    )
    return call(*operands, *earlier)


def chunk_widths(hidden_width):
    first = max(LANES, hidden_width // (2 * LANES) * LANES)
    return [first, hidden_width - first]


def round_up(value, step):
    return (value + step - 1) // step * step


def cut_kernel(gate, up, out, *, hidden_width, offset, wide):
    padded = round_up(wide, LANES)
    for owner in range(gate.shape[1] // hidden_width):
        column = owner * hidden_width + offset
        first = column // LANES * LANES
        shift = column - first
        span = round_up(shift + wide, LANES)
        for half, source in enumerate((gate, up)):
            part = source[:, first : first + span].astype(F32)
            if shift:
                part = pltpu.roll(part, span - shift, 1)
            if span < padded:
                part = jnp.concatenate([part, jnp.zeros((part.shape[0], padded - span), F32)], axis=1)
            part = part[:, :padded]
            if wide < padded:
                lane = lax.broadcasted_iota(jnp.int32, part.shape, 1)
                part = jnp.where(lane < wide, part, 0.0)
            out[owner, :, half * padded : (half + 1) * padded] = part.astype(BF)


def cut_gate_up(earlier, w_gate, w_up, hidden_width, offset, wide):
    rows, total = w_gate.shape
    whole = pl.BlockSpec(memory_space=pltpu.VMEM)
    out_shape = jax.ShapeDtypeStruct((total // hidden_width, rows, 2 * round_up(wide, LANES)), BF)
    kernel = functools.partial(cut_kernel, hidden_width=hidden_width, offset=offset, wide=wide)
    call = ordered_call(kernel, (w_gate, w_up), [whole] * 2, whole, out_shape, earlier, vmem=48)
    return call(w_gate, w_up, *earlier)


def swap_fsdp(values, mask):
    count = lax.axis_size("fsdp")
    return lax.ppermute(values, "fsdp", [(i, i ^ mask) for i in range(count)])


COVER = 10**12


def ordered_call(kernel, operands, in_specs, out_specs, out_shape, earlier, grid=(), scalars=0, scratch=(), vmem=16):
    count = scalars + len(operands)

    def body(*refs):
        kernel(*refs[:count], *refs[count + len(earlier) :])

    return pl.pallas_call(
        body,
        grid_spec=pltpu.PrefetchScalarGridSpec(
            num_scalar_prefetch=scalars,
            grid=grid,
            in_specs=list(in_specs) + [pl.BlockSpec(memory_space=pl.ANY)] * len(earlier),
            out_specs=out_specs,
            scratch_shapes=scratch,
        ),
        out_shape=out_shape,
        compiler_params=pltpu.CompilerParams(vmem_limit_bytes=vmem * 1024 * 1024),
        cost_estimate=pl.CostEstimate(flops=COVER, bytes_accessed=1024, transcendentals=0),
    )


def spacer_kernel(out):
    out[...] = jnp.zeros_like(out)


def spacer(earlier):
    out_shape = jax.ShapeDtypeStruct((8, LANES), F32)
    return ordered_call(spacer_kernel, (), [], pl.BlockSpec(memory_space=pltpu.VMEM), out_shape, earlier)(*earlier)


def place_kernel(index, *refs, sizes):
    count = len(sizes)
    pieces, out, semaphores = refs[:count], refs[count], refs[count + 1]
    copies = []
    for number, (mask, first, size) in enumerate(sizes):
        start = jnp.bitwise_xor(index[0], mask) * (out.shape[0] // 8) + first
        target = out.at[pl.ds(pl.multiple_of(start, 16), size)]
        copies.append(pltpu.make_async_copy(pieces[number], target, semaphores.at[number]))
        copies[-1].start()
    for copy in copies:
        copy.wait()


def place_parts(earlier, parts, index):
    if not isinstance(parts, list):
        return parts
    rows = sum(part.shape[0] for _, _, part in parts)
    columns, dtype = parts[0][2].shape[1], parts[0][2].dtype
    sizes = [(mask, first, part.shape[0]) for mask, first, part in parts]
    in_specs = [pl.BlockSpec(memory_space=pltpu.SMEM)] + [pl.BlockSpec(memory_space=pl.ANY)] * len(parts)
    out_specs = pl.BlockSpec(memory_space=pltpu.VMEM)
    out_shape = jax.ShapeDtypeStruct((rows, columns), dtype)
    operands = (index, *(part for _, _, part in parts))
    scratch = [pltpu.SemaphoreType.DMA((len(parts),))]
    kernel = functools.partial(place_kernel, sizes=sizes)
    call = ordered_call(kernel, operands, in_specs, out_specs, out_shape, earlier, scratch=scratch, vmem=32)
    return call(*operands, *earlier)


def gather_rows(rows):
    if lax.axis_size("fsdp") != 8:
        return (rows,), lax.all_gather(rows, "fsdp", axis=0, tiled=True)
    half = rows.shape[0] // 2
    from_x = swap_fsdp(rows, 2)
    from_y = swap_fsdp(rows, 4)
    far_first = swap_fsdp(from_y[:half], 2)
    far_last = swap_fsdp(from_x[half:], 4)
    parts = []
    for mask, first, part in ((0, 0, rows), (2, 0, from_x), (4, 0, from_y), (6, 0, far_first), (6, half, far_last)):
        parts.append((mask, first, part))
        parts.append((mask ^ 1, first, swap_fsdp(part, 1)))
    return (from_x, from_y), parts


def gather_small(rows):
    if lax.axis_size("fsdp") != 8:
        return lax.all_gather(rows, "fsdp", axis=0, tiled=True)
    found = [(mask, rows if mask == 0 else swap_fsdp(rows, mask)) for mask in (0, 2, 4, 6)]
    parts = [(mask, 0, part) for mask, part in found]
    parts += [(mask ^ 1, 0, swap_fsdp(part, 1)) for mask, part in found]
    return parts


def hold_kernel(values, out):
    out[...] = values[...]


def hold(earlier, values):
    whole = pl.BlockSpec(memory_space=pltpu.VMEM)
    out_shape = jax.ShapeDtypeStruct(values.shape, values.dtype)
    return ordered_call(hold_kernel, (values,), [whole], whole, out_shape, earlier)(values, *earlier)


def mask_kernel(values, valid, out):
    out[...] = (values[...].astype(F32) * valid[...]).astype(BF)


def mask_rows(earlier, values, valid):
    whole = pl.BlockSpec(memory_space=pltpu.VMEM)
    out_shape = jax.ShapeDtypeStruct(values.shape, BF)
    return ordered_call(mask_kernel, (values, valid), [whole] * 2, whole, out_shape, earlier)(values, valid, *earlier)


class Line:
    def __init__(self, ready):
        self.ready = ready
        self.marks = []
        self.last = ()

    def fence(self):
        small = self.last[0]
        small = small[(0,) * (small.ndim - 2)][:16, :LANES]
        self.last = (swap_fsdp(small, 1),)

    def kernel(self, call, *arrived):
        found = call(self.last + arrived)
        self.last = (jax.tree.leaves(found)[0],)
        return found

    def step(self, work, *arrived):
        ready = self.ready
        arrived = self.last + arrived

        def marked():
            return work(), [array[(0,) * (array.ndim - 1)][:1] for array in arrived]

        shapes = jax.eval_shape(marked)

        def skip():
            return jnp.logical_not(ready), jax.tree.map(lambda leaf: jnp.zeros(leaf.shape, leaf.dtype), shapes)

        self.ready, (found, marks) = lax.cond(ready, lambda: (ready, marked()), skip)
        self.marks += marks
        self.last = (jax.tree.leaves(found)[0],)
        self.kernel(spacer)
        return found


def add_kernel(left, right, out):
    out[...] = (left[...].astype(F32) + right[...].astype(F32)).astype(BF)


def add_low(earlier, left, right):
    shape = left.shape
    columns = shape[-1]
    left, right = left.reshape(-1, columns), right.reshape(-1, columns)
    total = left.shape[0]
    rows = next(size for size in (768, 512, 384, 256, 192, 128, 64, 32, 16, total) if total % size == 0)
    block = pl.BlockSpec((rows, columns), lambda step: (step, 0))
    out_shape = jax.ShapeDtypeStruct(left.shape, BF)
    call = ordered_call(add_kernel, (left, right), [block] * 2, block, out_shape, earlier, (total // rows,), vmem=32)
    return call(left, right, *earlier).reshape(shape)


def split_kernel(same, other, own, to_x, to_y, far_first, far_last):
    rows = own.shape[0]
    half = rows // 2
    for first, out in ((0, own), (rows, to_x), (2 * rows, to_y), (3 * rows, far_first), (3 * rows + half, far_last)):
        size = out.shape[0]
        left, right = same[first : first + size], other[first : first + size]
        out[...] = (left.astype(F32) + right.astype(F32)).astype(BF)


def far_masks(other):
    return (1, 3, 5, 7) if other else (0, 2, 4, 6)


def pick_shards(partial, other):
    if partial.shape[0] != 8:
        return partial.reshape(-1, partial.shape[2])
    index = lax.axis_index("fsdp")
    parts = [lax.dynamic_index_in_dim(partial, index ^ mask, 0, keepdims=False) for mask in far_masks(other)]
    return jnp.concatenate(parts, axis=0)


def from_core(other):
    return swap_fsdp(other, 1) if lax.axis_size("fsdp") == 8 else other


def split_sum(earlier, same, moved):
    if lax.axis_size("fsdp") != 8:
        return [lax.psum_scatter(same, "fsdp", scatter_dimension=0, tiled=True)]
    rows, columns = same.shape[0] // 4, same.shape[1]
    sizes = (rows, rows, rows, rows // 2, rows // 2)
    whole = pl.BlockSpec(memory_space=pltpu.VMEM)
    out_shape = [jax.ShapeDtypeStruct((size, columns), BF) for size in sizes]
    call = ordered_call(split_kernel, (same, moved), [whole] * 2, [whole] * 5, out_shape, earlier, vmem=32)
    return call(same, moved, *earlier)


def from_far(begun):
    return [swap_fsdp(begun[3], 2), swap_fsdp(begun[4], 4)] if len(begun) == 5 else begun


def mix_kernel(to_x, to_y, by_x, by_y, out_x, out_y):
    half = by_x.shape[0]
    out_x[:half] = to_x[:half]
    out_x[half:] = (to_x[half:].astype(F32) + by_y[...].astype(F32)).astype(BF)
    out_y[:half] = (to_y[:half].astype(F32) + by_x[...].astype(F32)).astype(BF)
    out_y[half:] = to_y[half:]


def mix_sum(earlier, begun, moved):
    if len(begun) != 5:
        return begun
    own, to_x, to_y = begun[:3]
    whole = pl.BlockSpec(memory_space=pltpu.VMEM)
    out_shape = [jax.ShapeDtypeStruct(to_x.shape, BF)] * 2
    operands = (to_x, to_y, *moved)
    call = ordered_call(mix_kernel, operands, [whole] * 4, [whole] * 2, out_shape, earlier, vmem=32)
    return [own] + list(call(*operands, *earlier))


def from_near(sent):
    return [sent[0], swap_fsdp(sent[1], 2), swap_fsdp(sent[2], 4)] if len(sent) == 3 else sent


def sum_kernel(*refs):
    total = refs[0][...].astype(F32)
    for part in refs[1:-1]:
        total = total + part[...].astype(F32)
    refs[-1][...] = total.astype(BF)


def sum_low(earlier, parts):
    whole = pl.BlockSpec(memory_space=pltpu.VMEM)
    out_shape = jax.ShapeDtypeStruct(parts[0].shape, BF)
    call = ordered_call(sum_kernel, tuple(parts), [whole] * len(parts), whole, out_shape, earlier, vmem=32)
    return call(*parts, *earlier)


def sum_parts(parts):
    total = parts[0].astype(F32)
    for part in parts[1:]:
        total = total + part.astype(F32)
    return total


def to_middle(values):
    return lax.ppermute(values, "sp", [(0, 1), (3, 2)])


def across_middle(values):
    return lax.ppermute(values, "sp", [(1, 2), (2, 1)])


def to_ends(values):
    return lax.ppermute(values, "sp", [(1, 0), (2, 3)])


def pick_sum(total, moved):
    place = lax.axis_index("sp")
    return jnp.where((place == 1) | (place == 2), total, moved)


def join_kernel(middle, *refs, hidden_width, widths):
    out = refs[-1]
    chunks = [refs[2 * n : 2 * n + 2] for n in range(len(widths))]
    total = out.shape[1]

    def fill(number):
        for owner in range(total // hidden_width):
            column = owner * hidden_width
            for chunk, wide in zip(chunks, widths):
                part = chunk[number][owner].astype(F32)
                first = column // LANES * LANES
                shift = column - first
                span = round_up(shift + wide, LANES)
                if span > part.shape[1]:
                    part = jnp.concatenate([part, jnp.zeros((part.shape[0], span - part.shape[1]), F32)], axis=1)
                if shift:
                    part = pltpu.roll(part, shift, 1)
                    lane = lax.broadcasted_iota(jnp.int32, (part.shape[0], LANES), 1)
                    head = jnp.where(lane >= shift, part[:, :LANES], out[:, first : first + LANES])
                    out[:, first : first + LANES] = head
                    if span > LANES:
                        out[:, first + LANES : first + span] = part[:, LANES:span]
                else:
                    out[:, first : first + span] = part[:, :span]
                column += wide

    @pl.when(middle[0] == 1)
    def _():
        fill(0)

    @pl.when(middle[0] == 0)
    def _():
        fill(1)


def join_columns(earlier, found, columns, hidden_width, widths):
    place = lax.axis_index("sp")
    middle = ((place == 1) | (place == 2)).astype(jnp.int32)[None]
    arrays = [part for chunk in found for part in chunk]
    count, total = arrays[0].shape[:2]
    rows = 16
    in_specs = [pl.BlockSpec(memory_space=pltpu.SMEM)]
    for wide, column in zip(widths, columns):
        block = pl.BlockSpec((count, rows, round_up(wide, LANES)), lambda block, column=column: (0, block, column))
        in_specs += [block, block]
    out_specs = pl.BlockSpec((rows, count * hidden_width), lambda block: (block, 0))
    out_shape = jax.ShapeDtypeStruct((total, count * hidden_width), F32)
    operands = (middle, *arrays)
    kernel = functools.partial(join_kernel, hidden_width=hidden_width, widths=widths)
    call = ordered_call(kernel, operands, in_specs, out_specs, out_shape, earlier, (total // rows,), vmem=32)
    return call(*operands, *earlier)


def stack_kernel(middle, *refs):
    out, chunks = refs[-1], refs[:-1]

    def fill(number):
        first = 0
        for n in range(len(chunks) // 2):
            rows = min(chunks[2 * n].shape[0], out.shape[0] - first)
            out[first : first + rows] = chunks[2 * n + number][:rows].astype(F32)
            first += rows

    @pl.when(middle[0] == 1)
    def _():
        fill(0)

    @pl.when(middle[0] == 0)
    def _():
        fill(1)


def stack_rows(earlier, found, rows):
    place = lax.axis_index("sp")
    middle = ((place == 1) | (place == 2)).astype(jnp.int32)[None]
    arrays = [part for chunk in found for part in chunk]
    whole = pl.BlockSpec(memory_space=pltpu.VMEM)
    in_specs = [pl.BlockSpec(memory_space=pltpu.SMEM)] + [whole] * len(arrays)
    out_shape = jax.ShapeDtypeStruct((rows, arrays[0].shape[1]), F32)
    operands = (middle, *arrays)
    return ordered_call(stack_kernel, operands, in_specs, whole, out_shape, earlier, vmem=40)(*operands, *earlier)


def activate_kernel(normed, grad, weights, down, hidden_out, grads_out, *, first):
    padded = weights.shape[1] // 2
    rows = normed[...]
    gate = product(rows, weights[:, :padded])
    up = product(rows, weights[:, padded:])
    hidden_grad = contract_last(grad[...], down[first : first + padded])
    sigma = 1.0 / (1.0 + jnp.exp(-gate))
    activated = gate * sigma
    hidden_out[...] = (activated * up).astype(BF)
    grads_out[:, :padded] = (hidden_grad * up * (sigma * (1.0 + gate * (1.0 - sigma)))).astype(BF)
    grads_out[:, padded:] = (hidden_grad * activated).astype(BF)


def activate(earlier, normed, grad, weights, down, first):
    total, width = normed.shape
    wide = weights.shape[1] // 2
    rows = 256
    by_rows = pl.BlockSpec((rows, width), lambda step: (step, 0))
    in_specs = [
        by_rows,
        by_rows,
        pl.BlockSpec(weights.shape, lambda step: (0, 0)),
        pl.BlockSpec(down.shape, lambda step: (0, 0)),
    ]
    out_specs = [pl.BlockSpec((rows, wide * n), lambda step: (step, 0)) for n in (1, 2)]
    out_shape = [jax.ShapeDtypeStruct((total, wide * n), BF) for n in (1, 2)]
    operands = (normed, grad, weights, down)
    kernel = functools.partial(activate_kernel, first=first)
    call = ordered_call(kernel, operands, in_specs, out_specs, out_shape, earlier, (total // rows,), vmem=56)
    return call(*operands, *earlier)


def back_kernel(order, grads_1, grads_2, weights_1, weights_2, out):
    total = contract_last(grads_1[...], weights_1[...]) + contract_last(grads_2[...], weights_2[...])
    out[...] = total.astype(BF)


def branch_kernel(order, hidden_1, hidden_2, down, out):
    first = hidden_1.shape[1]
    total = product(hidden_1[...], down[:first]) + product(hidden_2[...], down[first:])
    out[...] = total.astype(BF)


def row_products(earlier, kernel, lefts, rights, order, rows, width):
    blocks = order.shape[0]
    in_specs = [pl.BlockSpec((rows, part.shape[1]), lambda step, order_ref: (order_ref[step], 0)) for part in lefts]
    in_specs += [pl.BlockSpec(part.shape, lambda step, order_ref: (0, 0)) for part in rights]
    out_specs = pl.BlockSpec((rows, width), lambda step, order_ref: (step, 0))
    out_shape = jax.ShapeDtypeStruct((blocks * rows, width), BF)
    operands = (*lefts, *rights)
    call = ordered_call(kernel, operands, in_specs, out_specs, out_shape, earlier, (blocks,), scalars=1, vmem=56)
    return call(order, *operands, *earlier)


def per_device(
    tokens,
    cotangent,
    seq_lengths,
    block_order,
    w_query,
    w_key,
    w_value,
    b_query,
    b_key,
    b_value,
    w_output,
    gain_attn,
    gain_mlp,
    w_gate,
    w_up,
    w_down,
):
    local_rows, width = tokens.shape
    sp_count = lax.axis_size("sp")
    sp_index = lax.axis_index("sp")
    fsdp_count = lax.axis_size("fsdp")
    group_rows = local_rows * sp_count
    block_rows = local_rows // 2
    query_width = H * HD
    key_width = KVH * HD
    hidden_all = w_gate.shape[1]
    hidden_width = hidden_all // fsdp_count
    shard_rows = w_gate.shape[0]
    widths = chunk_widths(hidden_width)

    vector_parts = [b_query, b_key, b_value, gain_attn, gain_mlp]
    vector_sizes = [part.shape[0] for part in vector_parts]
    vector_size = sum(vector_sizes)
    kv_columns = 2 * key_width
    vector_rows = round_up(-(-vector_size // kv_columns), 16)
    vector_pad = jnp.zeros((vector_rows * kv_columns - vector_size,), BF)
    kv_shard = jnp.concatenate(
        [
            jnp.concatenate([w_key, w_value], axis=1),
            jnp.concatenate(vector_parts + [vector_pad]).reshape(vector_rows, kv_columns),
        ],
        axis=0,
    )
    fsdp_index = lax.axis_index("fsdp")
    own_index = fsdp_index[None]
    line = Line(seq_lengths[0] > 0)

    def exchange(cut):
        return lax.all_to_all(cut, "fsdp", split_axis=0, concat_axis=0, tiled=True).reshape(width, -1)

    def cut(first, wide, *arrived):
        return line.kernel(lambda earlier: cut_gate_up(earlier, w_gate, w_up, hidden_width, first, wide), *arrived)

    def place(parts, *arrived):
        return line.kernel(lambda earlier: place_parts(earlier, parts, own_index), *arrived)

    kv_parts = gather_small(kv_shard)
    q_hops, q_parts = gather_rows(line.kernel(lambda earlier: hold(earlier, w_query), kv_shard))
    kv_all = place(kv_parts)
    kv_all = kv_all.reshape(fsdp_count, -1, kv_columns)
    w_kv = kv_all[:, :shard_rows].reshape(width, kv_columns)
    vectors = kv_all[:, shard_rows:].reshape(fsdp_count, -1).astype(F32)
    edges = [sum(vector_sizes[:n]) for n in range(len(vector_sizes) + 1)]
    bias_q, bias_k, bias_v, gain_one, gain_two = (
        vectors[:, edges[n] : edges[n + 1]].reshape(-1) for n in range(len(vector_sizes))
    )
    order_row = block_order[0]
    local_pos = stream_positions(order_row, sp_index * local_rows, local_rows, block_rows)
    group_pos = stream_positions(order_row, 0, group_rows, block_rows)
    query_pos, key_pos = local_pos[:, None], group_pos[None, :]
    valid_rows = (local_pos < seq_lengths[0]).astype(F32)[:, None]
    upstream = cotangent.astype(F32)

    inputs = tokens.astype(F32)
    scale_one = lax.rsqrt(jnp.mean(inputs * inputs, axis=-1, keepdims=True) + EPS)
    unit_one = inputs * scale_one
    normed_one = (unit_one * gain_one).astype(BF)
    cosine, signed_sine = rotary_tables(local_pos)
    kv_lin = product(normed_one, w_kv)
    key_lin = kv_lin[:, :key_width] + bias_k
    key_rot = [
        (part * cosine + swap_halves(part) * signed_sine).astype(BF)
        for part in (key_lin[:, n * HD : (n + 1) * HD] for n in range(KVH))
    ]
    keys_values = jnp.concatenate(key_rot + [(kv_lin[:, key_width:] + bias_v).astype(BF)], axis=1)
    keys_values = lax.all_gather(keys_values, "sp", axis=0, tiled=True)
    o_hops, o_parts = gather_rows(line.kernel(lambda earlier: hold(earlier, w_output), *q_hops))
    w_q = place(q_parts)
    query_lin = product(normed_one, w_q) + bias_q
    grad_rows = line.kernel(lambda earlier: mask_rows(earlier, cotangent, valid_rows), *o_hops)
    grad_hops, grad_parts = gather_rows(grad_rows)
    weights_first = exchange(cut(0, widths[0]))
    query_rot, mixed = line.kernel(
        lambda earlier: attend_forward(earlier, query_lin, keys_values, cosine, signed_sine, query_pos, key_pos)
    )
    w_o = place(o_parts)
    attn_branch = product(mixed, w_o)
    hidden_in = inputs + valid_rows * attn_branch
    scale_two = lax.rsqrt(jnp.mean(hidden_in * hidden_in, axis=-1, keepdims=True) + EPS)
    unit_two = hidden_in * scale_two
    two_hops, two_parts = gather_rows((unit_two * gain_two).astype(BF))
    mlp_grad = place(grad_parts, weights_first, *two_hops)
    weights_last = exchange(cut(widths[0], widths[1]))
    normed_two = place(two_parts)

    def rows_exchange(half):
        return lax.all_to_all(half, "fsdp", split_axis=0, concat_axis=0, tiled=True)

    def weight_term(left, right):
        return contract_first(left, right).astype(BF)

    def by_rows(term):
        return term.reshape(fsdp_count, shard_rows, -1)

    def block_order(other):
        if fsdp_count != 8:
            return jnp.arange(fsdp_count, dtype=jnp.int32)
        return jnp.array(far_masks(other), jnp.int32) ^ fsdp_index

    first_wide, last_wide = (round_up(wide, LANES) for wide in widths)
    down = jnp.pad(w_down, ((0, first_wide + last_wide - hidden_width), (0, 0)))
    both_weights = [weights_first, weights_last]
    order_other, order_same = block_order(True), block_order(False)

    def weight_step(left, right, rows=True):
        def work():
            term = weight_term(left, right)
            return by_rows(term) if rows else term

        return line.step(work)

    def add(left, right, *arrived):
        return line.kernel(lambda earlier: add_low(earlier, left, right), *arrived)

    def split(same, moved, *arrived):
        return line.kernel(lambda earlier: split_sum(earlier, same, moved), *arrived)

    def mix(begun, moved, *arrived):
        return line.kernel(lambda earlier: mix_sum(earlier, begun, moved), *arrived)

    def row_step(kernel, lefts, rights, order, *arrived):
        return line.kernel(
            lambda earlier: row_products(earlier, kernel, lefts, rights, order, local_rows, width), *arrived
        )

    hidden_1, grads_1 = line.kernel(lambda earlier: activate(earlier, normed_two, mlp_grad, weights_first, down, 0))
    def both_step(left, right, wide):
        def work():
            term = weight_term(left, right)
            return by_rows(term[:, :wide]), by_rows(term[:, wide:])

        return line.step(work)

    gate_term_1, up_term_1 = both_step(normed_two, grads_1, first_wide)
    gate_1_in, up_1_in = to_middle(gate_term_1), to_middle(up_term_1)
    hidden_2, grads_2 = line.kernel(
        lambda earlier: activate(earlier, normed_two, mlp_grad, weights_last, down, first_wide)
    )
    gate_2, up_2 = grads_2[:, :last_wide], grads_2[:, last_wide:]
    grads = [grads_1, grads_2]
    gate_1_sum = add(gate_term_1, gate_1_in)
    gate_1_across = across_middle(gate_1_sum)
    back_other = row_step(back_kernel, grads, both_weights, order_other)
    back_moved = from_core(back_other)
    back_same = row_step(back_kernel, grads, both_weights, order_same)
    back_begun = split(back_same, back_moved)
    back_far = from_far(back_begun)
    up_1_sum = add(up_term_1, up_1_in)
    up_1_across = across_middle(up_1_sum)
    gate_1_total = rows_exchange(add(gate_1_sum, gate_1_across))
    down_1 = weight_step(hidden_1, mlp_grad, False)
    down_1_in = to_middle(down_1)
    back_sent = mix(back_begun, back_far)
    back_parts = from_near(back_sent)
    down_2 = weight_step(hidden_2, mlp_grad, False)
    up_1_total = add(up_1_sum, up_1_across, gate_1_total)
    gate_1_ends = to_ends(gate_1_total)
    up_1_total = rows_exchange(up_1_total)
    down_2_in = to_middle(down_2)
    branch = row_step(branch_kernel, [hidden_1, hidden_2], [down], jnp.arange(fsdp_count, dtype=jnp.int32))
    branch = lax.psum_scatter(branch, "fsdp", scatter_dimension=0, tiled=True)

    def norm_step():
        gain_grad, back = norm_backward(sum_parts(back_parts), unit_two, gain_two, scale_two)
        hidden_in_grad = upstream + back
        attn_grad = (valid_rows * hidden_in_grad).astype(BF)
        return gain_grad, hidden_in_grad, attn_grad, contract_last(attn_grad, w_o).astype(BF)

    gain_two_grad, hidden_in_grad, attn_grad, mixed_grad = line.step(norm_step)

    def attend_step(number, *arrived):
        query_grad, pair = line.kernel(
            lambda earlier: attend_backward(
                earlier, number, query_rot, mixed_grad, keys_values, cosine, signed_sine, query_pos, key_pos
            ),
            *arrived,
        )
        return query_grad, pair.reshape(sp_count, local_rows, 2 * HD)

    def pair_exchange(pair):
        return lax.all_to_all(pair, "sp", split_axis=0, concat_axis=0, tiled=True)

    down_1_sum = add(down_1, down_1_in, up_1_total, gate_1_ends)
    down_1_across = across_middle(down_1_sum)
    up_1_ends = to_ends(up_1_total)
    query_grad_0, pair_0 = attend_step(0)

    def scatter_weight(term):
        return lax.psum_scatter(term, "fsdp", scatter_dimension=0, tiled=True)

    down_2_sum = add(down_2, down_2_in)
    down_2_across = across_middle(down_2_sum)
    gate_term_2 = weight_step(normed_two, gate_2)
    gate_2_in = to_middle(gate_term_2)
    down_1_total = add(down_1_sum, down_1_across)
    down_1_ends = to_ends(down_1_total)
    output_term = line.step(lambda: weight_term(mixed, attn_grad), branch)
    output_share = scatter_weight(output_term)
    query_grad_1, pair_1 = attend_step(1)
    pairs = pair_exchange(jnp.concatenate([pair_0, pair_1], axis=2))
    gate_2_sum = add(gate_term_2, gate_2_in)
    gate_2_across = across_middle(gate_2_sum)
    line.fence()

    def kv_part(pair):
        pair_total = jnp.sum(pair.astype(F32), axis=0)
        part = pair_total[:, :HD]
        return (part * cosine - swap_halves(part) * signed_sine).astype(BF), pair_total[:, HD:].astype(BF)

    def query_step():
        query_lin_grad = jnp.concatenate([query_grad_0, query_grad_1], axis=1)
        sums = jnp.sum(query_lin_grad.astype(F32), axis=0)
        return weight_term(normed_one, query_lin_grad), contract_last(query_lin_grad, w_q), sums

    up_term_2 = weight_step(normed_two, up_2)
    up_2_in = to_middle(up_term_2)
    query_term, normed_one_first, query_sums = line.step(query_step)
    query_share = scatter_weight(query_term)
    down_2_total = add(down_2_sum, down_2_across)
    down_2_ends = to_ends(down_2_total)

    def held(values):
        return line.kernel(lambda earlier: hold(earlier, values))

    def kv_step():
        key_0, value_0 = kv_part(pairs[..., : 2 * HD])
        key_1, value_1 = kv_part(pairs[..., 2 * HD :])
        kv_lin_grad = jnp.concatenate([key_0, key_1, value_0, value_1], axis=1)
        normed_one_grad = normed_one_first + contract_last(kv_lin_grad, w_kv)
        gain_grad, back = norm_backward(normed_one_grad, unit_one, gain_one, scale_one)
        sums = jnp.sum(kv_lin_grad.astype(F32), axis=0)
        return weight_term(normed_one, kv_lin_grad), gain_grad, hidden_in_grad + back, sums

    kv_term, gain_one_grad, input_grad, kv_sums = line.step(kv_step)

    up_2_sum = add(up_term_2, up_2_in)
    up_2_across = across_middle(up_2_sum)
    gate_2_total = rows_exchange(add(gate_2_sum, gate_2_across, up_1_ends))

    def last_rows(vector):
        return vector.reshape(fsdp_count, -1)

    extra_rows = 32

    marks = line.marks

    def pack_step():
        mlp_branch = branch.astype(F32)
        result = hidden_in + valid_rows * mlp_branch
        stat_parts = jnp.stack(
            [
                jnp.sum(valid_rows * result * result),
                jnp.sum(valid_rows * attn_branch * attn_branch),
                jnp.sum(valid_rows * mlp_branch * mlp_branch),
                jnp.sum(valid_rows),
            ]
        )
        vector_sums = jnp.concatenate(
            [
                last_rows(query_sums),
                last_rows(kv_sums[:key_width]),
                last_rows(kv_sums[key_width:]),
                last_rows(gain_one_grad),
                last_rows(gain_two_grad),
                jnp.broadcast_to(stat_parts[None, :], (fsdp_count, 4)),
                jnp.broadcast_to(jnp.concatenate(marks)[None, :].astype(F32), (fsdp_count, len(marks))),
            ],
            axis=1,
        ).astype(BF)
        extra = jnp.pad(vector_sums, ((0, 0), (0, extra_rows * kv_columns - vector_sums.shape[1])))
        packed = jnp.concatenate(
            [
                kv_term.reshape(fsdp_count, shard_rows, kv_columns),
                extra.reshape(fsdp_count, extra_rows, kv_columns),
            ],
            axis=1,
        )
        return packed.reshape(-1, kv_columns), result.astype(BF)

    packed, layer_out = line.step(pack_step)
    kv_share = scatter_weight(packed)
    output_in = to_middle(output_share)
    down = (down_1_total, down_1_ends), (down_2_total, down_2_ends)
    grad_down = line.kernel(lambda earlier: stack_rows(earlier, down, hidden_width), gate_2_total)
    gate_2_ends = to_ends(gate_2_total)
    up_2_total = rows_exchange(add(up_2_sum, up_2_across))
    output_sum = add(output_share, output_in)
    output_across = across_middle(output_sum)
    query_share = held(query_share)
    query_in = to_middle(query_share)
    output_total = add(output_sum, output_across)
    output_ends = to_ends(output_total)
    gate = (gate_1_total, gate_1_ends), (gate_2_total, gate_2_ends)
    grad_gate = line.kernel(lambda earlier: join_columns(earlier, gate, (0, 0), hidden_width, widths))
    query_sum = add(query_share, query_in)
    query_across = across_middle(query_sum)

    def picked(total, moved):
        return line.kernel(lambda earlier: stack_rows(earlier, ((total, moved),), total.shape[0]))

    grad_output = picked(output_total, output_ends)
    kv_share = held(kv_share)
    kv_in = to_middle(kv_share)
    query_total = add(query_sum, query_across, up_2_total)
    up_2_ends = to_ends(up_2_total)
    query_ends = to_ends(query_total)
    kv_sum = add(kv_share, kv_in)
    kv_across = across_middle(kv_sum)
    kv_total = add(kv_sum, kv_across)
    kv_ends = to_ends(kv_total)
    grad_query = picked(query_total, query_ends)
    up = (up_1_total, up_1_ends), (up_2_total, up_2_ends)
    grad_up = line.kernel(lambda earlier: join_columns(earlier, up, (0, 0), hidden_width, widths))
    projections = picked(kv_total, kv_ends)
    sums = projections[shard_rows:].reshape(-1)
    grad_b_query, grad_b_key, grad_b_value, grad_gain_one, grad_gain_two = (
        sums[edges[n] : edges[n + 1]] for n in range(len(vector_sizes))
    )
    stats = sums[edges[-1] : edges[-1] + 4]
    root_means = jnp.sqrt(stats[:3] / (stats[3] * width))

    return (
        layer_out,
        input_grad,
        grad_query,
        projections[:shard_rows, :key_width],
        projections[:shard_rows, key_width:],
        grad_b_query,
        grad_b_key,
        grad_b_value,
        grad_output,
        grad_gain_one,
        grad_gain_two,
        grad_gate,
        grad_up,
        grad_down,
        root_means,
    )


def solution(mesh):
    both, first = P(("fsdp", "sp"), None), P("fsdp", None)
    one = P("fsdp")
    in_specs = (both, both, one, first, first, first, first, one, one, one, first, one, one, first, first, first)
    out_specs = (both, both, first, first, first, one, one, one, first, one, one, first, first, first, P())
    return jax.shard_map(per_device, mesh=mesh, in_specs=in_specs, out_specs=out_specs, check_vma=False)
```

```python
import functools

import jax
import jax.numpy as jnp
from jax import lax
from jax.experimental import pallas as pl
from jax.experimental.pallas import tpu as pltpu
from jax.sharding import PartitionSpec as P

H = 12
KVH = 2
HD = 128
HEADS_STEP = 2
LANES = 128


EPS = 1e-06
THETA = 1000000.0
BF = jnp.bfloat16
F32 = jnp.float32


def rotary_tables(positions):
    half_width = HD // 2
    inverse = THETA ** (-(jnp.arange(half_width, dtype=F32) * 2.0) / HD)
    angles = positions.astype(F32)[:, None] * inverse[None, :]
    cosine, sine = jnp.cos(angles), jnp.sin(angles)
    return (
        jnp.concatenate([cosine, cosine], axis=-1),
        jnp.concatenate([-sine, sine], axis=-1),
    )


def swap_halves(values):
    half_width = HD // 2
    return jnp.concatenate([values[..., half_width:], values[..., :half_width]], axis=-1)


def stream_positions(order_row, first_row, row_count, block_size):
    row_ids = first_row + jnp.arange(row_count, dtype=jnp.int32)
    which_block = row_ids // block_size
    matches = jnp.arange(order_row.shape[0], dtype=jnp.int32)[None, :] == which_block[:, None]
    block_start = jnp.sum(jnp.where(matches, order_row[None, :], 0), axis=1)
    return block_start * block_size + row_ids % block_size


def norm_backward(normed_grad, unit_rows, gain_rows, scale_rows):
    gain_grad = jnp.sum(normed_grad * unit_rows, axis=0)
    scaled = normed_grad * gain_rows
    inner = jnp.mean(scaled * unit_rows, axis=-1, keepdims=True)
    return (gain_grad, scale_rows * (scaled - unit_rows * inner))


def contract_last(left, right):
    return lax.dot_general(left, right, (((1,), (1,)), ((), ())), preferred_element_type=F32)


def contract_first(left, right):
    return lax.dot_general(left, right, (((0,), (0,)), ((), ())), preferred_element_type=F32)


def product(left, right):
    return jnp.dot(left, right, preferred_element_type=F32)


def head_scores(query, keys, allowed):
    scores = contract_last(query, keys) * (HD ** (-0.5))
    scores = jnp.where(allowed, scores, -1e30)
    weights_exp = jnp.exp(scores - jnp.max(scores, axis=-1, keepdims=True))
    return weights_exp, 1.0 / jnp.sum(weights_exp, axis=-1, keepdims=True)


def attend_forward_kernel(
    query_lin, keys, values, cosine, signed_sine, query_pos, key_pos, query_rot, mixed
):
    allowed = key_pos[...] <= query_pos[...]
    for head in range(HEADS_STEP):
        columns = slice(head * HD, (head + 1) * HD)
        linear = query_lin[:, columns]
        rotated = linear * cosine[...] + pltpu.roll(linear, HD // 2, 1) * signed_sine[...]
        rotated = rotated.astype(BF)
        query_rot[:, columns] = rotated
        weights_exp, inverse_sum = head_scores(rotated, keys[...], allowed)
        probabilities = (weights_exp * inverse_sum).astype(BF)
        mixed[:, columns] = product(probabilities, values[...]).astype(BF)


def attend_forward(earlier, query_lin, keys_values, cosine, signed_sine, query_pos, key_pos):
    rows, width = query_lin.shape
    count_all = keys_values.shape[0]
    per_kv = H // KVH // HEADS_STEP
    wide = HEADS_STEP * HD
    table = pl.BlockSpec((rows, HD), lambda step: (0, 0))
    by_head = pl.BlockSpec((rows, wide), lambda step: (0, step))
    in_specs = [
        by_head,
        pl.BlockSpec((count_all, HD), lambda step: (0, step // per_kv)),
        pl.BlockSpec((count_all, HD), lambda step: (0, KVH + step // per_kv)),
        table,
        table,
        pl.BlockSpec((rows, 1), lambda step: (0, 0)),
        pl.BlockSpec((1, count_all), lambda step: (0, 0)),
    ]
    out_shape = [jax.ShapeDtypeStruct((rows, width), BF)] * 2
    operands = (query_lin, keys_values, keys_values, cosine, signed_sine, query_pos, key_pos)
    call = ordered_call(
        attend_forward_kernel, operands, in_specs, [by_head, by_head], out_shape, earlier, (H // HEADS_STEP,), vmem=48
    )
    return call(*operands, *earlier)


def attend_backward_kernel(
    query_rot, out_grad, keys, values, cosine, signed_sine, query_pos, key_pos, query_grad, pair_grad, key_sum, value_sum
):
    step = pl.program_id(0)
    allowed = key_pos[...] <= query_pos[...]
    scaling = HD ** (-0.5)

    @pl.when(step == 0)
    def _():
        key_sum[...] = jnp.zeros_like(key_sum)
        value_sum[...] = jnp.zeros_like(value_sum)

    for head in range(HEADS_STEP):
        columns = slice(head * HD, (head + 1) * HD)
        query = query_rot[:, columns]
        grad = out_grad[:, columns]
        weights_exp, inverse_sum = head_scores(query, keys[...], allowed)
        probabilities = weights_exp * inverse_sum
        prob_grad = contract_last(grad, values[...])
        weighted = jnp.sum(probabilities * prob_grad, axis=-1, keepdims=True)
        score_grad = (probabilities * (prob_grad - weighted)).astype(BF)
        turned = product(score_grad, keys[...]) * scaling
        turned = turned * cosine[...] - pltpu.roll(turned, HD // 2, 1) * signed_sine[...]
        query_grad[:, columns] = turned.astype(BF)
        key_sum[...] += contract_first(score_grad, query) * scaling
        value_sum[...] += contract_first(probabilities.astype(BF), grad)

    @pl.when(step == pl.num_programs(0) - 1)
    def _():
        pair_grad[:, :HD] = key_sum[...].astype(BF)
        pair_grad[:, HD:] = value_sum[...].astype(BF)


def attend_backward(earlier, number, query_rot, out_grad, keys_values, cosine, signed_sine, query_pos, key_pos):
    rows = query_rot.shape[0]
    count_all = keys_values.shape[0]
    per_kv = H // KVH // HEADS_STEP
    wide = HEADS_STEP * HD
    table = pl.BlockSpec((rows, HD), lambda step: (0, 0))
    by_head = pl.BlockSpec((rows, wide), lambda step: (0, number * per_kv + step))
    in_specs = [
        by_head,
        by_head,
        pl.BlockSpec((count_all, HD), lambda step: (0, number)),
        pl.BlockSpec((count_all, HD), lambda step: (0, KVH + number)),
        table,
        table,
        pl.BlockSpec((rows, 1), lambda step: (0, 0)),
        pl.BlockSpec((1, count_all), lambda step: (0, 0)),
    ]
    out_specs = [
        pl.BlockSpec((rows, wide), lambda step: (0, step)),
        pl.BlockSpec((count_all, 2 * HD), lambda step: (0, 0)),
    ]
    out_shape = [
        jax.ShapeDtypeStruct((rows, per_kv * wide), BF),
        jax.ShapeDtypeStruct((count_all, 2 * HD), BF),
    ]
    operands = (query_rot, out_grad, keys_values, keys_values, cosine, signed_sine, query_pos, key_pos)
    scratch = [pltpu.VMEM((count_all, HD), F32)] * 2
    call = ordered_call(
        attend_backward_kernel, operands, in_specs, out_specs, out_shape, earlier, (per_kv,), scratch=scratch, vmem=48
    )
    return call(*operands, *earlier)


def chunk_widths(hidden_width):
    first = max(LANES, hidden_width // (2 * LANES) * LANES)
    return [first, hidden_width - first]


def round_up(value, step):
    return (value + step - 1) // step * step


def cut_kernel(gate, up, out, *, hidden_width, offset, wide):
    padded = round_up(wide, LANES)
    for owner in range(gate.shape[1] // hidden_width):
        column = owner * hidden_width + offset
        first = column // LANES * LANES
        shift = column - first
        span = round_up(shift + wide, LANES)
        for half, source in enumerate((gate, up)):
            part = source[:, first : first + span].astype(F32)
            if shift:
                part = pltpu.roll(part, span - shift, 1)
            if span < padded:
                part = jnp.concatenate([part, jnp.zeros((part.shape[0], padded - span), F32)], axis=1)
            part = part[:, :padded]
            if wide < padded:
                lane = lax.broadcasted_iota(jnp.int32, part.shape, 1)
                part = jnp.where(lane < wide, part, 0.0)
            out[owner, :, half * padded : (half + 1) * padded] = part.astype(BF)


def cut_gate_up(earlier, w_gate, w_up, hidden_width, offset, wide):
    rows, total = w_gate.shape
    whole = pl.BlockSpec(memory_space=pltpu.VMEM)
    out_shape = jax.ShapeDtypeStruct((total // hidden_width, rows, 2 * round_up(wide, LANES)), BF)
    kernel = functools.partial(cut_kernel, hidden_width=hidden_width, offset=offset, wide=wide)
    call = ordered_call(kernel, (w_gate, w_up), [whole] * 2, whole, out_shape, earlier, vmem=48)
    return call(w_gate, w_up, *earlier)


def swap_fsdp(values, mask):
    count = lax.axis_size("fsdp")
    return lax.ppermute(values, "fsdp", [(i, i ^ mask) for i in range(count)])


COVER = 10**12


def ordered_call(kernel, operands, in_specs, out_specs, out_shape, earlier, grid=(), scalars=0, scratch=(), vmem=16):
    count = scalars + len(operands)

    def body(*refs):
        kernel(*refs[:count], *refs[count + len(earlier) :])

    return pl.pallas_call(
        body,
        grid_spec=pltpu.PrefetchScalarGridSpec(
            num_scalar_prefetch=scalars,
            grid=grid,
            in_specs=list(in_specs) + [pl.BlockSpec(memory_space=pl.ANY)] * len(earlier),
            out_specs=out_specs,
            scratch_shapes=scratch,
        ),
        out_shape=out_shape,
        compiler_params=pltpu.CompilerParams(vmem_limit_bytes=vmem * 1024 * 1024),
        cost_estimate=pl.CostEstimate(flops=COVER, bytes_accessed=1024, transcendentals=0),
    )


def spacer_kernel(out):
    out[...] = jnp.zeros_like(out)


def spacer(earlier):
    out_shape = jax.ShapeDtypeStruct((8, LANES), F32)
    return ordered_call(spacer_kernel, (), [], pl.BlockSpec(memory_space=pltpu.VMEM), out_shape, earlier)(*earlier)


def place_kernel(index, *refs, sizes):
    count = len(sizes)
    pieces, out, semaphores = refs[:count], refs[count], refs[count + 1]
    copies = []
    for number, (mask, first, size) in enumerate(sizes):
        start = jnp.bitwise_xor(index[0], mask) * (out.shape[0] // 8) + first
        target = out.at[pl.ds(pl.multiple_of(start, 16), size)]
        copies.append(pltpu.make_async_copy(pieces[number], target, semaphores.at[number]))
        copies[-1].start()
    for copy in copies:
        copy.wait()


def place_parts(earlier, parts, index):
    if not isinstance(parts, list):
        return parts
    rows = sum(part.shape[0] for _, _, part in parts)
    columns, dtype = parts[0][2].shape[1], parts[0][2].dtype
    sizes = [(mask, first, part.shape[0]) for mask, first, part in parts]
    in_specs = [pl.BlockSpec(memory_space=pltpu.SMEM)] + [pl.BlockSpec(memory_space=pl.ANY)] * len(parts)
    out_specs = pl.BlockSpec(memory_space=pltpu.VMEM)
    out_shape = jax.ShapeDtypeStruct((rows, columns), dtype)
    operands = (index, *(part for _, _, part in parts))
    scratch = [pltpu.SemaphoreType.DMA((len(parts),))]
    kernel = functools.partial(place_kernel, sizes=sizes)
    call = ordered_call(kernel, operands, in_specs, out_specs, out_shape, earlier, scratch=scratch, vmem=32)
    return call(*operands, *earlier)


def gather_rows(rows):
    if lax.axis_size("fsdp") != 8:
        return (rows,), lax.all_gather(rows, "fsdp", axis=0, tiled=True)
    half = rows.shape[0] // 2
    from_x = swap_fsdp(rows, 2)
    from_y = swap_fsdp(rows, 4)
    far_first = swap_fsdp(from_y[:half], 2)
    far_last = swap_fsdp(from_x[half:], 4)
    parts = []
    for mask, first, part in ((0, 0, rows), (2, 0, from_x), (4, 0, from_y), (6, 0, far_first), (6, half, far_last)):
        parts.append((mask, first, part))
        parts.append((mask ^ 1, first, swap_fsdp(part, 1)))
    return (from_x, from_y), parts


def gather_small(rows):
    if lax.axis_size("fsdp") != 8:
        return lax.all_gather(rows, "fsdp", axis=0, tiled=True)
    found = [(mask, rows if mask == 0 else swap_fsdp(rows, mask)) for mask in (0, 2, 4, 6)]
    parts = [(mask, 0, part) for mask, part in found]
    parts += [(mask ^ 1, 0, swap_fsdp(part, 1)) for mask, part in found]
    return parts


def hold_kernel(values, out):
    out[...] = values[...]


def hold(earlier, values):
    whole = pl.BlockSpec(memory_space=pltpu.VMEM)
    out_shape = jax.ShapeDtypeStruct(values.shape, values.dtype)
    return ordered_call(hold_kernel, (values,), [whole], whole, out_shape, earlier)(values, *earlier)


def mask_kernel(values, valid, out):
    out[...] = (values[...].astype(F32) * valid[...]).astype(BF)


def mask_rows(earlier, values, valid):
    whole = pl.BlockSpec(memory_space=pltpu.VMEM)
    out_shape = jax.ShapeDtypeStruct(values.shape, BF)
    return ordered_call(mask_kernel, (values, valid), [whole] * 2, whole, out_shape, earlier)(values, valid, *earlier)


class Line:
    def __init__(self, ready):
        self.ready = ready
        self.marks = []
        self.last = ()

    def fence(self):
        small = self.last[0]
        small = small[(0,) * (small.ndim - 2)][:16, :LANES]
        self.last = (swap_fsdp(small, 1),)

    def kernel(self, call, *arrived):
        found = call(self.last + arrived)
        self.last = (jax.tree.leaves(found)[0],)
        return found

    def step(self, work, *arrived):
        ready = self.ready
        arrived = self.last + arrived

        def marked():
            return work(), [array[(0,) * (array.ndim - 1)][:1] for array in arrived]

        shapes = jax.eval_shape(marked)

        def skip():
            return jnp.logical_not(ready), jax.tree.map(lambda leaf: jnp.zeros(leaf.shape, leaf.dtype), shapes)

        self.ready, (found, marks) = lax.cond(ready, lambda: (ready, marked()), skip)
        self.marks += marks
        self.last = (jax.tree.leaves(found)[0],)
        self.kernel(spacer)
        return found


def add_kernel(left, right, out):
    out[...] = (left[...].astype(F32) + right[...].astype(F32)).astype(BF)


def add_low(earlier, left, right):
    shape = left.shape
    columns = shape[-1]
    left, right = left.reshape(-1, columns), right.reshape(-1, columns)
    total = left.shape[0]
    rows = next(size for size in (768, 512, 384, 256, 192, 128, 64, 32, 16, total) if total % size == 0)
    block = pl.BlockSpec((rows, columns), lambda step: (step, 0))
    out_shape = jax.ShapeDtypeStruct(left.shape, BF)
    call = ordered_call(add_kernel, (left, right), [block] * 2, block, out_shape, earlier, (total // rows,), vmem=32)
    return call(left, right, *earlier).reshape(shape)


def split_kernel(same, other, own, to_x, to_y, far_first, far_last):
    rows = own.shape[0]
    half = rows // 2
    for first, out in ((0, own), (rows, to_x), (2 * rows, to_y), (3 * rows, far_first), (3 * rows + half, far_last)):
        size = out.shape[0]
        left, right = same[first : first + size], other[first : first + size]
        out[...] = (left.astype(F32) + right.astype(F32)).astype(BF)


def far_masks(other):
    return (1, 3, 5, 7) if other else (0, 2, 4, 6)


def pick_shards(partial, other):
    if partial.shape[0] != 8:
        return partial.reshape(-1, partial.shape[2])
    index = lax.axis_index("fsdp")
    parts = [lax.dynamic_index_in_dim(partial, index ^ mask, 0, keepdims=False) for mask in far_masks(other)]
    return jnp.concatenate(parts, axis=0)


def from_core(other):
    return swap_fsdp(other, 1) if lax.axis_size("fsdp") == 8 else other


def split_sum(earlier, same, moved):
    if lax.axis_size("fsdp") != 8:
        return [lax.psum_scatter(same, "fsdp", scatter_dimension=0, tiled=True)]
    rows, columns = same.shape[0] // 4, same.shape[1]
    sizes = (rows, rows, rows, rows // 2, rows // 2)
    whole = pl.BlockSpec(memory_space=pltpu.VMEM)
    out_shape = [jax.ShapeDtypeStruct((size, columns), BF) for size in sizes]
    call = ordered_call(split_kernel, (same, moved), [whole] * 2, [whole] * 5, out_shape, earlier, vmem=32)
    return call(same, moved, *earlier)


def from_far(begun):
    return [swap_fsdp(begun[3], 2), swap_fsdp(begun[4], 4)] if len(begun) == 5 else begun


def mix_kernel(to_x, to_y, by_x, by_y, out_x, out_y):
    half = by_x.shape[0]
    out_x[:half] = to_x[:half]
    out_x[half:] = (to_x[half:].astype(F32) + by_y[...].astype(F32)).astype(BF)
    out_y[:half] = (to_y[:half].astype(F32) + by_x[...].astype(F32)).astype(BF)
    out_y[half:] = to_y[half:]


def mix_sum(earlier, begun, moved):
    if len(begun) != 5:
        return begun
    own, to_x, to_y = begun[:3]
    whole = pl.BlockSpec(memory_space=pltpu.VMEM)
    out_shape = [jax.ShapeDtypeStruct(to_x.shape, BF)] * 2
    operands = (to_x, to_y, *moved)
    call = ordered_call(mix_kernel, operands, [whole] * 4, [whole] * 2, out_shape, earlier, vmem=32)
    return [own] + list(call(*operands, *earlier))


def from_near(sent):
    return [sent[0], swap_fsdp(sent[1], 2), swap_fsdp(sent[2], 4)] if len(sent) == 3 else sent


def sum_kernel(*refs):
    total = refs[0][...].astype(F32)
    for part in refs[1:-1]:
        total = total + part[...].astype(F32)
    refs[-1][...] = total.astype(BF)


def sum_low(earlier, parts):
    whole = pl.BlockSpec(memory_space=pltpu.VMEM)
    out_shape = jax.ShapeDtypeStruct(parts[0].shape, BF)
    call = ordered_call(sum_kernel, tuple(parts), [whole] * len(parts), whole, out_shape, earlier, vmem=32)
    return call(*parts, *earlier)


def sum_parts(parts):
    total = parts[0].astype(F32)
    for part in parts[1:]:
        total = total + part.astype(F32)
    return total


def to_middle(values):
    return lax.ppermute(values, "sp", [(0, 1), (3, 2)])


def across_middle(values):
    return lax.ppermute(values, "sp", [(1, 2), (2, 1)])


def to_ends(values):
    return lax.ppermute(values, "sp", [(1, 0), (2, 3)])


def pick_sum(total, moved):
    place = lax.axis_index("sp")
    return jnp.where((place == 1) | (place == 2), total, moved)


def join_kernel(middle, *refs, hidden_width, widths):
    out = refs[-1]
    chunks = [refs[2 * n : 2 * n + 2] for n in range(len(widths))]
    total = out.shape[1]

    def fill(number):
        for owner in range(total // hidden_width):
            column = owner * hidden_width
            for chunk, wide in zip(chunks, widths):
                part = chunk[number][owner].astype(F32)
                first = column // LANES * LANES
                shift = column - first
                span = round_up(shift + wide, LANES)
                if span > part.shape[1]:
                    part = jnp.concatenate([part, jnp.zeros((part.shape[0], span - part.shape[1]), F32)], axis=1)
                if shift:
                    part = pltpu.roll(part, shift, 1)
                    lane = lax.broadcasted_iota(jnp.int32, (part.shape[0], LANES), 1)
                    head = jnp.where(lane >= shift, part[:, :LANES], out[:, first : first + LANES])
                    out[:, first : first + LANES] = head
                    if span > LANES:
                        out[:, first + LANES : first + span] = part[:, LANES:span]
                else:
                    out[:, first : first + span] = part[:, :span]
                column += wide

    @pl.when(middle[0] == 1)
    def _():
        fill(0)

    @pl.when(middle[0] == 0)
    def _():
        fill(1)


def join_columns(earlier, found, columns, hidden_width, widths):
    place = lax.axis_index("sp")
    middle = ((place == 1) | (place == 2)).astype(jnp.int32)[None]
    arrays = [part for chunk in found for part in chunk]
    count, total = arrays[0].shape[:2]
    rows = 16
    in_specs = [pl.BlockSpec(memory_space=pltpu.SMEM)]
    for wide, column in zip(widths, columns):
        block = pl.BlockSpec((count, rows, round_up(wide, LANES)), lambda block, column=column: (0, block, column))
        in_specs += [block, block]
    out_specs = pl.BlockSpec((rows, count * hidden_width), lambda block: (block, 0))
    out_shape = jax.ShapeDtypeStruct((total, count * hidden_width), F32)
    operands = (middle, *arrays)
    kernel = functools.partial(join_kernel, hidden_width=hidden_width, widths=widths)
    call = ordered_call(kernel, operands, in_specs, out_specs, out_shape, earlier, (total // rows,), vmem=32)
    return call(*operands, *earlier)


def stack_kernel(middle, *refs):
    out, chunks = refs[-1], refs[:-1]

    def fill(number):
        first = 0
        for n in range(len(chunks) // 2):
            rows = min(chunks[2 * n].shape[0], out.shape[0] - first)
            out[first : first + rows] = chunks[2 * n + number][:rows].astype(F32)
            first += rows

    @pl.when(middle[0] == 1)
    def _():
        fill(0)

    @pl.when(middle[0] == 0)
    def _():
        fill(1)


def stack_rows(earlier, found, rows):
    place = lax.axis_index("sp")
    middle = ((place == 1) | (place == 2)).astype(jnp.int32)[None]
    arrays = [part for chunk in found for part in chunk]
    whole = pl.BlockSpec(memory_space=pltpu.VMEM)
    in_specs = [pl.BlockSpec(memory_space=pltpu.SMEM)] + [whole] * len(arrays)
    out_shape = jax.ShapeDtypeStruct((rows, arrays[0].shape[1]), F32)
    operands = (middle, *arrays)
    return ordered_call(stack_kernel, operands, in_specs, whole, out_shape, earlier, vmem=40)(*operands, *earlier)


def activate_kernel(normed, grad, weights, down, hidden_out, grads_out, *, first):
    padded = weights.shape[1] // 2
    rows = normed[...]
    gate = product(rows, weights[:, :padded])
    up = product(rows, weights[:, padded:])
    hidden_grad = contract_last(grad[...], down[first : first + padded])
    sigma = 1.0 / (1.0 + jnp.exp(-gate))
    activated = gate * sigma
    hidden_out[...] = (activated * up).astype(BF)
    grads_out[:, :padded] = (hidden_grad * up * (sigma * (1.0 + gate * (1.0 - sigma)))).astype(BF)
    grads_out[:, padded:] = (hidden_grad * activated).astype(BF)


def activate(earlier, normed, grad, weights, down, first):
    total, width = normed.shape
    wide = weights.shape[1] // 2
    rows = 256
    by_rows = pl.BlockSpec((rows, width), lambda step: (step, 0))
    in_specs = [
        by_rows,
        by_rows,
        pl.BlockSpec(weights.shape, lambda step: (0, 0)),
        pl.BlockSpec(down.shape, lambda step: (0, 0)),
    ]
    out_specs = [pl.BlockSpec((rows, wide * n), lambda step: (step, 0)) for n in (1, 2)]
    out_shape = [jax.ShapeDtypeStruct((total, wide * n), BF) for n in (1, 2)]
    operands = (normed, grad, weights, down)
    kernel = functools.partial(activate_kernel, first=first)
    call = ordered_call(kernel, operands, in_specs, out_specs, out_shape, earlier, (total // rows,), vmem=56)
    return call(*operands, *earlier)


def back_kernel(order, grads_1, grads_2, weights_1, weights_2, out):
    total = contract_last(grads_1[...], weights_1[...]) + contract_last(grads_2[...], weights_2[...])
    out[...] = total.astype(BF)


def branch_kernel(order, hidden_1, hidden_2, down, out):
    first = hidden_1.shape[1]
    total = product(hidden_1[...], down[:first]) + product(hidden_2[...], down[first:])
    out[...] = total.astype(BF)


def row_products(earlier, kernel, lefts, rights, order, rows, width):
    blocks = order.shape[0]
    in_specs = [pl.BlockSpec((rows, part.shape[1]), lambda step, order_ref: (order_ref[step], 0)) for part in lefts]
    in_specs += [pl.BlockSpec(part.shape, lambda step, order_ref: (0, 0)) for part in rights]
    out_specs = pl.BlockSpec((rows, width), lambda step, order_ref: (step, 0))
    out_shape = jax.ShapeDtypeStruct((blocks * rows, width), BF)
    operands = (*lefts, *rights)
    call = ordered_call(kernel, operands, in_specs, out_specs, out_shape, earlier, (blocks,), scalars=1, vmem=56)
    return call(order, *operands, *earlier)


def per_device(
    tokens,
    cotangent,
    seq_lengths,
    block_order,
    w_query,
    w_key,
    w_value,
    b_query,
    b_key,
    b_value,
    w_output,
    gain_attn,
    gain_mlp,
    w_gate,
    w_up,
    w_down,
):
    local_rows, width = tokens.shape
    sp_count = lax.axis_size("sp")
    sp_index = lax.axis_index("sp")
    fsdp_count = lax.axis_size("fsdp")
    group_rows = local_rows * sp_count
    block_rows = local_rows // 2
    query_width = H * HD
    key_width = KVH * HD
    hidden_all = w_gate.shape[1]
    hidden_width = hidden_all // fsdp_count
    shard_rows = w_gate.shape[0]
    widths = chunk_widths(hidden_width)

    vector_parts = [b_query, b_key, b_value, gain_attn, gain_mlp]
    vector_sizes = [part.shape[0] for part in vector_parts]
    vector_size = sum(vector_sizes)
    kv_columns = 2 * key_width
    vector_rows = round_up(-(-vector_size // kv_columns), 16)
    vector_pad = jnp.zeros((vector_rows * kv_columns - vector_size,), BF)
    kv_shard = jnp.concatenate(
        [
            jnp.concatenate([w_key, w_value], axis=1),
            jnp.concatenate(vector_parts + [vector_pad]).reshape(vector_rows, kv_columns),
        ],
        axis=0,
    )
    fsdp_index = lax.axis_index("fsdp")
    own_index = fsdp_index[None]
    line = Line(seq_lengths[0] > 0)

    def exchange(cut):
        return lax.all_to_all(cut, "fsdp", split_axis=0, concat_axis=0, tiled=True).reshape(width, -1)

    def cut(first, wide, *arrived):
        return line.kernel(lambda earlier: cut_gate_up(earlier, w_gate, w_up, hidden_width, first, wide), *arrived)

    def place(parts, *arrived):
        return line.kernel(lambda earlier: place_parts(earlier, parts, own_index), *arrived)

    kv_parts = gather_small(kv_shard)
    q_hops, q_parts = gather_rows(line.kernel(lambda earlier: hold(earlier, w_query), kv_shard))
    kv_all = place(kv_parts)
    kv_all = kv_all.reshape(fsdp_count, -1, kv_columns)
    w_kv = kv_all[:, :shard_rows].reshape(width, kv_columns)
    vectors = kv_all[:, shard_rows:].reshape(fsdp_count, -1).astype(F32)
    edges = [sum(vector_sizes[:n]) for n in range(len(vector_sizes) + 1)]
    bias_q, bias_k, bias_v, gain_one, gain_two = (
        vectors[:, edges[n] : edges[n + 1]].reshape(-1) for n in range(len(vector_sizes))
    )
    order_row = block_order[0]
    local_pos = stream_positions(order_row, sp_index * local_rows, local_rows, block_rows)
    group_pos = stream_positions(order_row, 0, group_rows, block_rows)
    query_pos, key_pos = local_pos[:, None], group_pos[None, :]
    valid_rows = (local_pos < seq_lengths[0]).astype(F32)[:, None]
    upstream = cotangent.astype(F32)

    inputs = tokens.astype(F32)
    scale_one = lax.rsqrt(jnp.mean(inputs * inputs, axis=-1, keepdims=True) + EPS)
    unit_one = inputs * scale_one
    normed_one = (unit_one * gain_one).astype(BF)
    cosine, signed_sine = rotary_tables(local_pos)
    kv_lin = product(normed_one, w_kv)
    key_lin = kv_lin[:, :key_width] + bias_k
    key_rot = [
        (part * cosine + swap_halves(part) * signed_sine).astype(BF)
        for part in (key_lin[:, n * HD : (n + 1) * HD] for n in range(KVH))
    ]
    keys_values = jnp.concatenate(key_rot + [(kv_lin[:, key_width:] + bias_v).astype(BF)], axis=1)
    keys_values = lax.all_gather(keys_values, "sp", axis=0, tiled=True)
    o_hops, o_parts = gather_rows(line.kernel(lambda earlier: hold(earlier, w_output), *q_hops))
    w_q = place(q_parts)
    query_lin = product(normed_one, w_q) + bias_q
    grad_rows = line.kernel(lambda earlier: mask_rows(earlier, cotangent, valid_rows), *o_hops)
    grad_hops, grad_parts = gather_rows(grad_rows)
    weights_first = exchange(cut(0, widths[0]))
    query_rot, mixed = line.kernel(
        lambda earlier: attend_forward(earlier, query_lin, keys_values, cosine, signed_sine, query_pos, key_pos)
    )
    w_o = place(o_parts)
    attn_branch = product(mixed, w_o)
    hidden_in = inputs + valid_rows * attn_branch
    scale_two = lax.rsqrt(jnp.mean(hidden_in * hidden_in, axis=-1, keepdims=True) + EPS)
    unit_two = hidden_in * scale_two
    two_hops, two_parts = gather_rows((unit_two * gain_two).astype(BF))
    mlp_grad = place(grad_parts, weights_first, *two_hops)
    weights_last = exchange(cut(widths[0], widths[1]))
    normed_two = place(two_parts)

    def rows_exchange(half):
        return lax.all_to_all(half, "fsdp", split_axis=0, concat_axis=0, tiled=True)

    def weight_term(left, right):
        return contract_first(left, right).astype(BF)

    def by_rows(term):
        return term.reshape(fsdp_count, shard_rows, -1)

    def block_order(other):
        if fsdp_count != 8:
            return jnp.arange(fsdp_count, dtype=jnp.int32)
        return jnp.array(far_masks(other), jnp.int32) ^ fsdp_index

    first_wide, last_wide = (round_up(wide, LANES) for wide in widths)
    down = jnp.pad(w_down, ((0, first_wide + last_wide - hidden_width), (0, 0)))
    both_weights = [weights_first, weights_last]
    order_other, order_same = block_order(True), block_order(False)

    def weight_step(left, right, rows=True):
        def work():
            term = weight_term(left, right)
            return by_rows(term) if rows else term

        return line.step(work)

    def add(left, right, *arrived):
        return line.kernel(lambda earlier: add_low(earlier, left, right), *arrived)

    def split(same, moved, *arrived):
        return line.kernel(lambda earlier: split_sum(earlier, same, moved), *arrived)

    def mix(begun, moved, *arrived):
        return line.kernel(lambda earlier: mix_sum(earlier, begun, moved), *arrived)

    def row_step(kernel, lefts, rights, order, *arrived):
        return line.kernel(
            lambda earlier: row_products(earlier, kernel, lefts, rights, order, local_rows, width), *arrived
        )

    hidden_1, grads_1 = line.kernel(lambda earlier: activate(earlier, normed_two, mlp_grad, weights_first, down, 0))
    def both_step(left, right, wide):
        def work():
            term = weight_term(left, right)
            return by_rows(term[:, :wide]), by_rows(term[:, wide:])

        return line.step(work)

    gate_term_1, up_term_1 = both_step(normed_two, grads_1, first_wide)
    gate_1_in, up_1_in = to_middle(gate_term_1), to_middle(up_term_1)
    hidden_2, grads_2 = line.kernel(
        lambda earlier: activate(earlier, normed_two, mlp_grad, weights_last, down, first_wide)
    )
    gate_2, up_2 = grads_2[:, :last_wide], grads_2[:, last_wide:]
    grads = [grads_1, grads_2]
    gate_1_sum = add(gate_term_1, gate_1_in)
    gate_1_across = across_middle(gate_1_sum)
    back_other = row_step(back_kernel, grads, both_weights, order_other)
    back_moved = from_core(back_other)
    back_same = row_step(back_kernel, grads, both_weights, order_same)
    back_begun = split(back_same, back_moved)
    back_far = from_far(back_begun)
    up_1_sum = add(up_term_1, up_1_in)
    up_1_across = across_middle(up_1_sum)
    gate_1_total = rows_exchange(add(gate_1_sum, gate_1_across))
    down_1 = weight_step(hidden_1, mlp_grad, False)
    down_1_in = to_middle(down_1)
    back_sent = mix(back_begun, back_far)
    back_parts = from_near(back_sent)
    down_2 = weight_step(hidden_2, mlp_grad, False)
    up_1_total = add(up_1_sum, up_1_across, gate_1_total)
    gate_1_ends = to_ends(gate_1_total)
    up_1_total = rows_exchange(up_1_total)
    down_2_in = to_middle(down_2)
    branch = row_step(branch_kernel, [hidden_1, hidden_2], [down], jnp.arange(fsdp_count, dtype=jnp.int32))
    branch = lax.psum_scatter(branch, "fsdp", scatter_dimension=0, tiled=True)

    def norm_step():
        gain_grad, back = norm_backward(sum_parts(back_parts), unit_two, gain_two, scale_two)
        hidden_in_grad = upstream + back
        attn_grad = (valid_rows * hidden_in_grad).astype(BF)
        return gain_grad, hidden_in_grad, attn_grad, contract_last(attn_grad, w_o).astype(BF)

    gain_two_grad, hidden_in_grad, attn_grad, mixed_grad = line.step(norm_step)

    def attend_step(number, *arrived):
        query_grad, pair = line.kernel(
            lambda earlier: attend_backward(
                earlier, number, query_rot, mixed_grad, keys_values, cosine, signed_sine, query_pos, key_pos
            ),
            *arrived,
        )
        return query_grad, pair.reshape(sp_count, local_rows, 2 * HD)

    def pair_exchange(pair):
        return lax.all_to_all(pair, "sp", split_axis=0, concat_axis=0, tiled=True)

    down_1_sum = add(down_1, down_1_in, up_1_total, gate_1_ends)
    down_1_across = across_middle(down_1_sum)
    up_1_ends = to_ends(up_1_total)
    query_grad_0, pair_0 = attend_step(0)

    def scatter_weight(term):
        return lax.psum_scatter(term, "fsdp", scatter_dimension=0, tiled=True)

    down_2_sum = add(down_2, down_2_in)
    down_2_across = across_middle(down_2_sum)
    gate_term_2 = weight_step(normed_two, gate_2)
    gate_2_in = to_middle(gate_term_2)
    down_1_total = add(down_1_sum, down_1_across)
    down_1_ends = to_ends(down_1_total)
    output_term = line.step(lambda: weight_term(mixed, attn_grad), branch)
    output_share = scatter_weight(output_term)
    query_grad_1, pair_1 = attend_step(1)
    pairs = pair_exchange(jnp.concatenate([pair_0, pair_1], axis=2))
    gate_2_sum = add(gate_term_2, gate_2_in)
    gate_2_across = across_middle(gate_2_sum)
    line.fence()

    def kv_part(pair):
        pair_total = jnp.sum(pair.astype(F32), axis=0)
        part = pair_total[:, :HD]
        return (part * cosine - swap_halves(part) * signed_sine).astype(BF), pair_total[:, HD:].astype(BF)

    def query_step():
        query_lin_grad = jnp.concatenate([query_grad_0, query_grad_1], axis=1)
        sums = jnp.sum(query_lin_grad.astype(F32), axis=0)
        return weight_term(normed_one, query_lin_grad), contract_last(query_lin_grad, w_q), sums

    up_term_2 = weight_step(normed_two, up_2)
    up_2_in = to_middle(up_term_2)
    query_term, normed_one_first, query_sums = line.step(query_step)
    query_share = scatter_weight(query_term)
    down_2_total = add(down_2_sum, down_2_across)
    down_2_ends = to_ends(down_2_total)

    def held(values):
        return line.kernel(lambda earlier: hold(earlier, values))

    def kv_step():
        key_0, value_0 = kv_part(pairs[..., : 2 * HD])
        key_1, value_1 = kv_part(pairs[..., 2 * HD :])
        kv_lin_grad = jnp.concatenate([key_0, key_1, value_0, value_1], axis=1)
        normed_one_grad = normed_one_first + contract_last(kv_lin_grad, w_kv)
        gain_grad, back = norm_backward(normed_one_grad, unit_one, gain_one, scale_one)
        sums = jnp.sum(kv_lin_grad.astype(F32), axis=0)
        return weight_term(normed_one, kv_lin_grad), gain_grad, hidden_in_grad + back, sums

    kv_term, gain_one_grad, input_grad, kv_sums = line.step(kv_step)

    up_2_sum = add(up_term_2, up_2_in)
    up_2_across = across_middle(up_2_sum)
    gate_2_total = rows_exchange(add(gate_2_sum, gate_2_across, up_1_ends))

    def last_rows(vector):
        return vector.reshape(fsdp_count, -1)

    extra_rows = 32

    marks = line.marks

    def pack_step():
        mlp_branch = branch.astype(F32)
        result = hidden_in + valid_rows * mlp_branch
        stat_parts = jnp.stack(
            [
                jnp.sum(valid_rows * result * result),
                jnp.sum(valid_rows * attn_branch * attn_branch),
                jnp.sum(valid_rows * mlp_branch * mlp_branch),
                jnp.sum(valid_rows),
            ]
        )
        vector_sums = jnp.concatenate(
            [
                last_rows(query_sums),
                last_rows(kv_sums[:key_width]),
                last_rows(kv_sums[key_width:]),
                last_rows(gain_one_grad),
                last_rows(gain_two_grad),
                jnp.broadcast_to(stat_parts[None, :], (fsdp_count, 4)),
                jnp.broadcast_to(jnp.concatenate(marks)[None, :].astype(F32), (fsdp_count, len(marks))),
            ],
            axis=1,
        ).astype(BF)
        extra = jnp.pad(vector_sums, ((0, 0), (0, extra_rows * kv_columns - vector_sums.shape[1])))
        packed = jnp.concatenate(
            [
                kv_term.reshape(fsdp_count, shard_rows, kv_columns),
                extra.reshape(fsdp_count, extra_rows, kv_columns),
            ],
            axis=1,
        )
        return packed.reshape(-1, kv_columns), result.astype(BF)

    packed, layer_out = line.step(pack_step)
    kv_share = scatter_weight(packed)
    output_in = to_middle(output_share)
    output_sum = add(output_share, output_in)
    output_across = across_middle(output_sum)
    down = (down_1_total, down_1_ends), (down_2_total, down_2_ends)
    grad_down = line.kernel(lambda earlier: stack_rows(earlier, down, hidden_width), gate_2_total)
    gate_2_ends = to_ends(gate_2_total)
    up_2_total = rows_exchange(add(up_2_sum, up_2_across))
    query_share = held(query_share)
    query_in = to_middle(query_share)
    output_total = add(output_sum, output_across)
    output_ends = to_ends(output_total)
    gate = (gate_1_total, gate_1_ends), (gate_2_total, gate_2_ends)
    grad_gate = line.kernel(lambda earlier: join_columns(earlier, gate, (0, 0), hidden_width, widths))
    query_sum = add(query_share, query_in)
    query_across = across_middle(query_sum)

    def picked(total, moved):
        return line.kernel(lambda earlier: stack_rows(earlier, ((total, moved),), total.shape[0]))

    grad_output = picked(output_total, output_ends)
    kv_share = held(kv_share)
    kv_in = to_middle(kv_share)
    query_total = add(query_sum, query_across, up_2_total)
    up_2_ends = to_ends(up_2_total)
    query_ends = to_ends(query_total)
    kv_sum = add(kv_share, kv_in)
    kv_across = across_middle(kv_sum)
    kv_total = add(kv_sum, kv_across)
    kv_ends = to_ends(kv_total)
    grad_query = picked(query_total, query_ends)
    up = (up_1_total, up_1_ends), (up_2_total, up_2_ends)
    grad_up = line.kernel(lambda earlier: join_columns(earlier, up, (0, 0), hidden_width, widths))
    projections = picked(kv_total, kv_ends)
    sums = projections[shard_rows:].reshape(-1)
    grad_b_query, grad_b_key, grad_b_value, grad_gain_one, grad_gain_two = (
        sums[edges[n] : edges[n + 1]] for n in range(len(vector_sizes))
    )
    stats = sums[edges[-1] : edges[-1] + 4]
    root_means = jnp.sqrt(stats[:3] / (stats[3] * width))

    return (
        layer_out,
        input_grad,
        grad_query,
        projections[:shard_rows, :key_width],
        projections[:shard_rows, key_width:],
        grad_b_query,
        grad_b_key,
        grad_b_value,
        grad_output,
        grad_gain_one,
        grad_gain_two,
        grad_gate,
        grad_up,
        grad_down,
        root_means,
    )


def solution(mesh):
    both, first = P(("fsdp", "sp"), None), P("fsdp", None)
    one = P("fsdp")
    in_specs = (both, both, one, first, first, first, first, one, one, one, first, one, one, first, first, first)
    out_specs = (both, both, first, first, first, one, one, one, first, one, one, first, first, first, P())
    return jax.shard_map(per_device, mesh=mesh, in_specs=in_specs, out_specs=out_specs, check_vma=False)
```
